256 devices in a mesh: inst: 4 (over y_lo, core), dom: 64 (over x, y_hi, z).
Axes of the slice: x: 4, y: 4 (y_hi: 2, y_lo: 2; y = y_hi * 2 + y_lo), z: 8, core: 2. Of those that a mesh axis runs over, the one named last changes fastest.
Arguments:
- state: float32 [8, 40, 8192], P('inst', None, 'dom'), may hold values from -6 to 6
- element_jacobian_blocks: float32 [8, 40, 40, 8192], P('inst', None, None, 'dom'), may hold values from -1 to 1
- face_blocks: float32 [8, 20, 20, 49152], P('inst', None, None, 'dom'), may hold values from -1.25 to 1.25
- mass: float32 [8, 8192], P(None, 'dom'), may hold values from 0.3 to 3
- counts: int32 [64], P('dom'), may hold values from 64 to 128, as said below
- face_owner: int32 [49152], P('dom'), may hold values from 0 to 127, as said below
- face_side: int32 [49152], P('dom'), may hold values from 0 to 5
- face_part: int32 [49152], P('dom'), may hold values from 0 to 63, as said below
- face_nbr: int32 [49152], P('dom'), may hold values from 0 to 127, as said below
Outputs:
- first: float32 [8, 40, 8192], P('inst', None, 'dom')
- second: float32 [8, 40, 8192], P('inst', None, 'dom')
The draws below stay inside these ranges and needn't reach their ends.
Inputs may be any that keep to these rules, and one draw needn't show every extreme that they name: `counts`: some partition uses all 128 slots. `face_owner`: below the count of the entry's partition. `face_part`: differs from the entry's partition by -2, -1, 0, 1 or 2 around the closed loop of 64 partitions; of one partition's entries each of the four other partitions so reached is named by 64 to 128 of them, and in every partition one of them by exactly 128. `face_nbr`: below the count of the neighbour's partition.
All inputs are finite; a program needn't handle non-finite values.
Results may differ from the reference program's by a relative error of at most 0.00008.
Values sent between devices are 32-bit elements; how exact they have to be, the bound alone decides.
No kernel may reach another device: no remote copies, remote signals or barrier semaphores. Data moves between devices by JAX's collectives and lax.ppermute only.
A program may use at most 128 MiB of HBM per device.

```python
import math
import jax
import jax.numpy as jnp
from jax import lax

INST = 8
E_DEV = 128
F_DEV = 768
PARTS_SIZE = 64
ELEMS = 8192
FACES = 49152


def face_graph(key):
    count_key, load_key, pick_key, order_key, owner_key, destination_key, side_key = jax.random.split(key, 7)
    drawn_counts = jax.random.randint(count_key, (PARTS_SIZE,), E_DEV // 2, E_DEV + 1)
    full_part = jax.random.randint(jax.random.fold_in(count_key, 9), (), 0, PARTS_SIZE)
    element_counts = drawn_counts.at[full_part].set(E_DEV)
    burden = jax.random.randint(load_key, (PARTS_SIZE, 4), E_DEV // 2, E_DEV + 1)
    chosen = jax.random.randint(pick_key, (PARTS_SIZE,), 0, 4)
    burden = jnp.where(jnp.arange(4)[None, :] == chosen[:, None], E_DEV, burden)
    limits = jnp.cumsum(burden, axis=1)
    position = jnp.arange(F_DEV)
    bucket = jnp.sum((position[None, :, None] >= limits[:, None, :]).astype(jnp.int32), axis=2)
    shifts = jnp.array([-2, -1, 1, 2, 0], jnp.int32)
    offset_in = shifts[bucket]
    part_keys = jax.random.split(order_key, PARTS_SIZE)
    shuffle = jax.vmap(lambda child_key: jax.random.permutation(child_key, F_DEV))(part_keys)
    offset_in = jnp.take_along_axis(offset_in, shuffle, axis=1)
    home_part = jnp.arange(PARTS_SIZE, dtype=jnp.int32)[:, None]
    partner = jnp.mod(home_part + offset_in, PARTS_SIZE)
    owner_rows = jax.random.randint(owner_key, (PARTS_SIZE, F_DEV), 0, element_counts[:, None])
    neighbour_rows = jax.random.randint(destination_key, (PARTS_SIZE, F_DEV), 0, element_counts[partner])
    face_sides = jax.random.randint(side_key, (PARTS_SIZE, F_DEV), 0, 6)
    return (element_counts, owner_rows.reshape(-1), face_sides.reshape(-1), partner.reshape(-1), neighbour_rows.reshape(-1))


def draw_counts(key, part):
    return face_graph(key)[0]


def draw_face_owner(key, part):
    return face_graph(key)[1]


def draw_face_side(key, part):
    return face_graph(key)[2]


def draw_face_part(key, part):
    return face_graph(key)[3]


def draw_face_nbr(key, part):
    return face_graph(key)[4]


def level_of(rng, shape, pieces, low, top_value):
    level, own = 1.0, jax.random.fold_in(rng, 6)
    for dim, parts in pieces:
        draws = jnp.exp(jax.random.uniform(jax.random.fold_in(own, dim), (parts,), jnp.float32, low / len(pieces), top_value / len(pieces)))
        level = level * jnp.repeat(draws, shape[dim] // parts).reshape([-1 if axis == dim else 1 for axis in range(len(shape))])
    return level


def gaussian(key, dims, spread, most, cuts=(), held_as=jnp.bfloat16):
    values = spread * jax.random.normal(key, dims, jnp.float32)
    if cuts:
        values = values * level_of(key, dims, cuts, -0.22, 0.18)
    return jnp.clip(values, -most, most).astype(held_as)


def setup_inputs(seed: int = 0) -> dict:
    seeds = jax.random.split(jax.random.key(seed), 10)
    return {
        "state": gaussian(seeds[0], (INST, 40, ELEMS), 1.0, 6.0, ((0, 4), (2, 64)), jnp.float32),
        "element_jacobian_blocks": gaussian(seeds[1], (INST, 40, 40, ELEMS), 40 ** -0.5, 1.0, ((0, 4), (3, 64)), jnp.float32),
        "face_blocks": gaussian(seeds[2], (INST, 20, 20, FACES), 20 ** -0.5, 1.25, ((0, 4), (3, 64)), jnp.float32),
        "mass": jnp.clip(jnp.exp(math.log(3.0) - 2.3025851 * jax.random.uniform(seeds[3], (8, ELEMS), jnp.float32) ** level_of(seeds[3], (8, ELEMS), ((1, 64),), -0.2, 0.2)), 0.3, 3.0),
        "counts": draw_counts(jax.random.fold_in(seeds[9], 71), 0),
        "face_owner": draw_face_owner(jax.random.fold_in(seeds[9], 71), 0),
        "face_side": draw_face_side(jax.random.fold_in(seeds[9], 71), 0),
        "face_part": draw_face_part(jax.random.fold_in(seeds[9], 71), 0),
        "face_nbr": draw_face_nbr(jax.random.fold_in(seeds[9], 71), 0),
    }


TOP_PRECISION = lax.Precision.HIGHEST
OMEGA = 1.0


def spectral_table(total):
    entries = []
    for target in range(total):
        row_values = []
        for source in range(total):
            spacing = target - source
            wrapped = spacing % total
            if wrapped != 0 and 2 * wrapped != total:
                row_values.append(0.5 * OMEGA * (-1.0) ** spacing / math.tan(math.pi * spacing / total))
            else:
                row_values.append(0.0)
        entries.append(row_values)
    return jnp.asarray(entries, dtype=jnp.float32)


def trace_rows():
    result = []
    for side in range(6):
        corners = [corner for corner in range(8) if (corner >> (side // 2)) & 1 == side % 2]
        row_values = []
        for variable in range(5):
            for within in range(4):
                row_values.append(variable * 8 + corners[within])
        result.append(row_values)
    return result


def face_index(sides):
    lookup = jnp.asarray(trace_rows(), dtype=jnp.int32)
    matched = (sides[:, None] == jnp.arange(6, dtype=jnp.int32)[None, :]).astype(jnp.int32)
    return jnp.dot(matched, lookup)


def extract(states, columns, sides):
    picked = jnp.take(states, columns, axis=2)
    row_index = jnp.transpose(face_index(sides))[None, :, :]
    return jnp.take_along_axis(picked, row_index, axis=1)


def reference(state, element_jacobian_blocks, face_blocks, mass, counts, face_owner, face_side, face_part, face_nbr):
    slots = jnp.arange(ELEMS, dtype=jnp.int32)
    live = (slots % E_DEV < counts[slots // E_DEV]).astype(jnp.float32)
    entry_part = jnp.arange(FACES, dtype=jnp.int32) // F_DEV
    owner_cols = entry_part * E_DEV + face_owner
    neighbour_cols = face_part * E_DEV + face_nbr
    owner_rows = jnp.transpose(face_index(face_side))
    owner_grid = jnp.broadcast_to(owner_cols[None, :], owner_rows.shape)
    far_sides = jnp.bitwise_xor(face_side, 1)
    coupling = spectral_table(INST)
    mass_rows = jnp.tile(mass, (5, 1))

    def apply_jacobian(vector):
        element_term = jnp.einsum("tije,tje->tie", element_jacobian_blocks, vector, precision=TOP_PRECISION)
        traces = extract(vector, neighbour_cols, far_sides)
        across = jnp.einsum("tijf,tjf->tif", face_blocks, traces, precision=TOP_PRECISION)
        face_contribution = jnp.zeros_like(vector).at[:, owner_rows, owner_grid].add(across)
        time_term = mass_rows * jnp.einsum("ts,sre->tre", coupling, vector, precision=TOP_PRECISION)
        return live * (element_term + face_contribution + time_term)

    first = apply_jacobian(state * live)
    second = apply_jacobian(first)
    return first, second
```

```python
import functools
import math

import jax
import jax.numpy as jnp
from jax import lax
from jax.experimental import pallas as pl
from jax.experimental.pallas import tpu as pltpu
from jax.sharding import PartitionSpec as P

OMEGA = 1.0
OFFSETS = (-2, -1, 1, 2)


def spectral(spacing, total):
    wrapped = spacing % total
    if wrapped == 0 or 2 * wrapped == total:
        return 0.0
    return 0.5 * OMEGA * (-1.0) ** wrapped / math.tan(math.pi * wrapped / total)


def pull(value, axis, offset):
    length = lax.axis_size(axis)
    return lax.ppermute(value, axis, [((i + offset) % length, i) for i in range(length)])


def sublanes():
    return lax.broadcasted_iota(jnp.int32, (8, 128), 0)


def fold_rows(tiles):
    row = sublanes()
    step = 1
    while len(tiles) > 1:
        keep = (row & step) == 0
        merged = []
        for first, second in zip(tiles[0::2], tiles[1::2]):
            own = jnp.where(keep, first, second)
            other = jnp.where(keep, second, first)
            merged.append(own + pltpu.roll(other, 8 - step, 0))
        tiles = merged
        step *= 2
    return tiles[0]


def element_kernel(vector_ref, blocks_ref, out_ref):
    insts, unknowns, _ = vector_ref.shape
    for t in range(insts):
        tiles = [vector_ref[t, 8 * g : 8 * g + 8, :] for g in range(unknowns // 8)]
        for group in range(unknowns // 8):
            partial = []
            for i in range(8 * group, 8 * group + 8):
                total = blocks_ref[t, i, 0:8, :] * tiles[0]
                for g in range(1, unknowns // 8):
                    total += blocks_ref[t, i, 8 * g : 8 * g + 8, :] * tiles[g]
                partial.append(total)
            out_ref[t, 8 * group : 8 * group + 8, :] = fold_rows(partial)


def element_term(vector, blocks):
    return pl.pallas_call(
        element_kernel,
        out_shape=jax.ShapeDtypeStruct(vector.shape, jnp.float32),
        in_specs=[pl.BlockSpec(memory_space=pltpu.VMEM)] * 2,
        out_specs=pl.BlockSpec(memory_space=pltpu.VMEM),
        cost_estimate=pl.CostEstimate(
            flops=2 * blocks.size, bytes_accessed=4 * blocks.size, transcendentals=0
        ),
        compiler_params=pltpu.CompilerParams(vmem_limit_bytes=32 * 2**20),
    )(vector, blocks)


def corner_of(side, within):
    axis, end = side >> 1, side & 1
    return jnp.where(
        axis == 0,
        2 * within + end,
        jnp.where(
            axis == 1,
            (within & 1) + 2 * end + 4 * (within >> 1),
            4 * end + within,
        ),
    )


def within_of(side, corner):
    axis, end = side >> 1, side & 1
    place = jnp.where(
        axis == 0,
        corner >> 1,
        jnp.where(axis == 1, (corner & 1) + 2 * (corner >> 2), corner & 3),
    )
    held = ((corner >> axis) & 1) == end
    return place, held


def face_kernel(
    instances,
    part_total,
    counts_ref,
    my_ref,
    owner_ref,
    side_ref,
    part_ref,
    nbr_ref,
    mass_ref,
    element_ref,
    blocks_ref,
    own_ref,
    *rest,
):
    neighbour_refs = rest[: len(OFFSETS)]
    instance_refs = rest[len(OFFSETS) : len(OFFSETS) + instances - 1]
    out_ref, trace_ref, across_ref, spread_ref = rest[len(OFFSETS) + instances - 1 :]
    insts, unknowns, elements = own_ref.shape
    variables = unknowns // 8
    width = 4 * variables
    lane_tiles = owner_ref.shape[0]
    stride = lane_tiles * insts
    row = sublanes()
    shape = (8, 128)

    def wide(ref, tile):
        return jnp.broadcast_to(ref[tile : tile + 1, :], shape)

    for tile in range(lane_tiles):
        column = wide(nbr_ref, tile)
        offset = wide(part_ref, tile) - my_ref[0]
        offset = jnp.where(offset > 2, offset - part_total, offset)
        offset = jnp.where(offset < -2, offset + part_total, offset)
        chosen = [offset == o for o in OFFSETS]
        corner = corner_of(wide(side_ref, tile) ^ 1, row & 3)
        for t in range(insts):
            traces = []
            for a in range(variables):
                rows = slice(8 * a, 8 * a + 8)
                picked = jnp.take_along_axis(
                    own_ref[t, rows, :], column, axis=1, mode="promise_in_bounds"
                )
                for mask, ref in zip(chosen, neighbour_refs):
                    picked = jnp.where(
                        mask,
                        jnp.take_along_axis(
                            ref[t, rows, :], column, axis=1, mode="promise_in_bounds"
                        ),
                        picked,
                    )
                traces.append(
                    jnp.take_along_axis(picked, corner, axis=0, mode="promise_in_bounds")
                )
            for a in range(0, variables, 2):
                start = 4 * a * stride + tile * insts + t
                if a + 1 < variables:
                    pair = jnp.where(row < 4, traces[a], traces[a + 1])
                    trace_ref[pl.ds(start, 8, stride=stride), :] = pair
                else:
                    trace_ref[pl.ds(start, 4, stride=stride), :] = traces[a][0:4, :]

    pair_rows = 2 * stride
    for i in range(width):
        total = None
        for p in range(width // 2):
            base = (i * width + 2 * p) * stride
            term = (
                blocks_ref[base : base + pair_rows, :]
                * trace_ref[p * pair_rows : (p + 1) * pair_rows, :]
            )
            total = term if total is None else total + term
        across_ref[i * pair_rows : (i + 1) * pair_rows, :] = total

    for tile in range(lane_tiles):
        place, held = within_of(wide(side_ref, tile), row)
        for t in range(insts):
            for a in range(variables):
                start = 4 * (a // 2) * 2 * pair_rows + tile * insts + t
                if a % 2 == 0:
                    here = across_ref[pl.ds(start, 8, stride=pair_rows), :]
                    here += across_ref[pl.ds(start + stride, 8, stride=pair_rows), :]
                moved = jnp.take_along_axis(
                    here, place + 4 * (a % 2), axis=0, mode="promise_in_bounds"
                )
                spread_ref[
                    (t * variables + a) * 8 : (t * variables + a) * 8 + 8,
                    tile * 128 : tile * 128 + 128,
                ] = jnp.where(held, moved, 0.0)

    slot = lax.broadcasted_iota(jnp.int32, (elements, 128), 0)
    owned = jnp.concatenate(
        [
            (jnp.broadcast_to(owner_ref[tile : tile + 1, :], slot.shape) == slot)
            for tile in range(lane_tiles)
        ],
        axis=1,
    )
    owned = jnp.where(owned, 1.0, 0.0).astype(jnp.bfloat16)
    spread = spread_ref[...]
    high = spread.astype(jnp.bfloat16)
    low = (spread - high.astype(jnp.float32)).astype(jnp.bfloat16)
    dims = (((1,), (1,)), ((), ()))
    landed = lax.dot_general(high, owned, dims, preferred_element_type=jnp.float32)
    landed += lax.dot_general(low, owned, dims, preferred_element_type=jnp.float32)

    live = lax.broadcasted_iota(jnp.int32, shape, 1) < counts_ref[0]
    mass = mass_ref[...]
    total_insts = insts * instances
    sources = (own_ref, *instance_refs)
    for t in range(insts):
        for a in range(variables):
            rows = slice(8 * a, 8 * a + 8)
            summed = None
            for k, ref in enumerate(sources):
                for s in range(insts):
                    weight = spectral(t - s - insts * k, total_insts)
                    if weight != 0.0:
                        term = weight * ref[s, rows, :]
                        summed = term if summed is None else summed + term
            base = (t * variables + a) * 8
            value = element_ref[t, rows, :] + landed[base : base + 8, :] + mass * summed
            out_ref[t, rows, :] = jnp.where(live, value, 0.0)


def face_and_time_term(
    counts, my_part, owner, side, part, nbr, mass, element, blocks, own, neighbours, others
):
    part_total = lax.axis_size("dom")
    instances = lax.axis_size("inst")
    insts, unknowns, _ = own.shape
    width = unknowns // 2
    stride = owner.shape[0] * insts
    vmem = pl.BlockSpec(memory_space=pltpu.VMEM)
    smem = pl.BlockSpec(memory_space=pltpu.SMEM)
    return pl.pallas_call(
        functools.partial(face_kernel, instances, part_total),
        out_shape=jax.ShapeDtypeStruct(own.shape, jnp.float32),
        in_specs=[smem, smem] + [vmem] * (8 + len(neighbours) + len(others)),
        out_specs=vmem,
        scratch_shapes=[
            pltpu.VMEM((width * stride, 128), jnp.float32),
            pltpu.VMEM(((width + 4) * 2 * stride, 128), jnp.float32),
            pltpu.VMEM((insts * unknowns, owner.shape[0] * 128), jnp.float32),
        ],
        cost_estimate=pl.CostEstimate(
            flops=2 * blocks.size, bytes_accessed=4 * blocks.size, transcendentals=0
        ),
        compiler_params=pltpu.CompilerParams(vmem_limit_bytes=32 * 2**20),
    )(counts, my_part, owner, side, part, nbr, mass, element, blocks, own, *neighbours, *others)


def on_device(
    state,
    element_jacobian_blocks,
    face_blocks,
    mass,
    counts,
    face_owner,
    face_side,
    face_part,
    face_nbr,
):
    insts, rows, columns, faces = face_blocks.shape
    tiles = faces // 128
    blocks = face_blocks.reshape(insts, rows, columns, tiles, 128)
    blocks = jnp.transpose(blocks, (1, 2, 3, 0, 4)).reshape(-1, 128)
    owner, side, part, nbr = (
        x.reshape(tiles, 128) for x in (face_owner, face_side, face_part, face_nbr)
    )
    my_part = lax.axis_index("dom").astype(jnp.int32).reshape(1)

    def apply_jacobian(vector):
        neighbours = [pull(vector, "dom", o) for o in OFFSETS]
        others = [pull(vector, "inst", k) for k in range(1, lax.axis_size("inst"))]
        element = element_term(vector, element_jacobian_blocks)
        return face_and_time_term(
            counts, my_part, owner, side, part, nbr, mass, element, blocks, vector,
            neighbours, others,
        )

    first = apply_jacobian(state)
    second = apply_jacobian(first)
    return first, second


def solution(mesh):
    placed = (
        P("inst", None, "dom"),
        P("inst", None, None, "dom"),
        P("inst", None, None, "dom"),
        P(None, "dom"),
        P("dom"),
        P("dom"),
        P("dom"),
        P("dom"),
        P("dom"),
    )
    return jax.shard_map(
        on_device,
        mesh=mesh,
        in_specs=placed,
        out_specs=(P("inst", None, "dom"), P("inst", None, "dom")),
        check_vma=False,
    )
```

```python
import functools
import math

import jax
import jax.numpy as jnp
from jax import lax
from jax.experimental import pallas as pl
from jax.experimental.pallas import tpu as pltpu
from jax.sharding import PartitionSpec as P

OMEGA = 1.0


def spectral(spacing, total):
    wrapped = spacing % total
    if wrapped == 0 or 2 * wrapped == total:
        return 0.0
    return 0.5 * OMEGA * (-1.0) ** wrapped / math.tan(math.pi * wrapped / total)


def joint(rule):
    insts, parts = lax.axis_size("inst"), lax.axis_size("dom")
    pairs = []
    for inst in range(insts):
        for part in range(parts):
            to_inst, to_part = rule(inst, part)
            pairs.append((inst * parts + part, to_inst * parts + to_part % parts))
    return pairs


def send(value, rule):
    return lax.ppermute(value, ("inst", "dom"), joint(rule))


def to_core(inst, part):
    return inst ^ 1, part


def to_chip(inst, part):
    return inst ^ 2, part


def near_step(part, reach):
    return -reach if part & reach else reach


def to_near(inst, part):
    return inst, part + near_step(part, 1 + inst % 2)


def to_far(inst, part):
    return inst, part - near_step(part, 1 + inst % 2)


def pack_kernel(own_ref, other_ref, out_ref):
    insts = own_ref.shape[0]
    out_ref[:insts] = own_ref[...]
    out_ref[insts:] = other_ref[...]


def pack(own, other):
    return pl.pallas_call(
        pack_kernel,
        out_shape=jax.ShapeDtypeStruct((2 * own.shape[0],) + own.shape[1:], jnp.float32),
        in_specs=[pl.BlockSpec(memory_space=pltpu.VMEM)] * 2,
        out_specs=pl.BlockSpec(memory_space=pltpu.VMEM),
        cost_estimate=pl.CostEstimate(flops=0, bytes_accessed=16 * own.size, transcendentals=0),
        compiler_params=pltpu.CompilerParams(vmem_limit_bytes=2**20),
    )(own, other)


def sublanes():
    return lax.broadcasted_iota(jnp.int32, (8, 128), 0)


def fold_rows(tiles):
    row = sublanes()
    step = 1
    while len(tiles) > 1:
        keep = (row & step) == 0
        merged = []
        for first, second in zip(tiles[0::2], tiles[1::2]):
            own = jnp.where(keep, first, second)
            other = jnp.where(keep, second, first)
            merged.append(own + pltpu.roll(other, 8 - step, 0))
        tiles = merged
        step *= 2
    return tiles[0]


def element_term(vector_ref, blocks_ref, t):
    unknowns = vector_ref.shape[1]
    tiles = [vector_ref[t, 8 * g : 8 * g + 8, :] for g in range(unknowns // 8)]
    groups = []
    for group in range(unknowns // 8):
        partial = []
        for i in range(8 * group, 8 * group + 8):
            total = blocks_ref[t, i, 0:8, :] * tiles[0]
            for g in range(1, unknowns // 8):
                total += blocks_ref[t, i, 8 * g : 8 * g + 8, :] * tiles[g]
            partial.append(total)
        groups.append(fold_rows(partial))
    return groups


def regroup_kernel(blocks_ref, out_ref):
    rows, columns, insts, faces = blocks_ref.shape
    lane_tiles = faces // 128
    stride = lane_tiles * insts

    def one_row(i, carry):
        base = pl.multiple_of(i * columns * stride, 8)
        for p in range(columns):
            for tile in range(lane_tiles):
                out_ref[pl.ds(base + p * stride + tile * insts, insts), :] = blocks_ref[
                    i, p, :, tile * 128 : tile * 128 + 128
                ]
        return carry

    lax.fori_loop(0, rows, one_row, 0)


def regroup(blocks):
    return pl.pallas_call(
        regroup_kernel,
        out_shape=jax.ShapeDtypeStruct((blocks.size // 128, 128), jnp.float32),
        in_specs=[pl.BlockSpec(memory_space=pltpu.VMEM)],
        out_specs=pl.BlockSpec(memory_space=pltpu.VMEM),
        cost_estimate=pl.CostEstimate(
            flops=0, bytes_accessed=8 * blocks.size, transcendentals=0
        ),
        compiler_params=pltpu.CompilerParams(vmem_limit_bytes=16 * 2**20),
    )(blocks)


def corner_of(side, within):
    axis, end = side >> 1, side & 1
    return jnp.where(
        axis == 0,
        2 * within + end,
        jnp.where(
            axis == 1,
            (within & 1) + 2 * end + 4 * (within >> 1),
            4 * end + within,
        ),
    )


def within_of(side, corner):
    axis, end = side >> 1, side & 1
    place = jnp.where(
        axis == 0,
        corner >> 1,
        jnp.where(axis == 1, (corner & 1) + 2 * (corner >> 2), corner & 3),
    )
    held = ((corner >> axis) & 1) == end
    return place, held


def jacobian_kernel(
    instances,
    part_total,
    counts_ref,
    place_ref,
    owner_ref,
    side_ref,
    part_ref,
    nbr_ref,
    mass_ref,
    element_blocks_ref,
    blocks_ref,
    own_ref,
    core_ref,
    chip_ref,
    far_ref,
    near_ref,
    other_far_ref,
    other_near_ref,
    out_ref,
    trace_ref,
    across_ref,
    spread_ref,
):
    my_part = place_ref[0]
    on_first = place_ref[1] == 0
    step_one = jnp.where((my_part & 1) == 0, 1, -1)
    step_two = jnp.where((my_part & 2) == 0, 2, -2)
    mine = jnp.where(on_first, step_one, step_two)
    others = jnp.where(on_first, step_two, step_one)
    neighbours = (
        (-mine, far_ref, 0),
        (mine, near_ref, 0),
        (-others, other_far_ref, 1),
        (others, other_near_ref, 1),
    )
    insts, unknowns, elements = own_ref.shape
    variables = unknowns // 8
    width = 4 * variables
    lane_tiles = owner_ref.shape[0]
    stride = lane_tiles * insts
    row = sublanes()
    shape = (8, 128)

    def wide(ref, tile):
        return jnp.broadcast_to(ref[tile : tile + 1, :], shape)

    for tile in range(lane_tiles):
        column = wide(nbr_ref, tile)
        offset = wide(part_ref, tile) - my_part
        offset = jnp.where(offset > 2, offset - part_total, offset)
        offset = jnp.where(offset < -2, offset + part_total, offset)
        chosen = [offset == o for o, _, _ in neighbours]
        corner = corner_of(wide(side_ref, tile) ^ 1, row & 3)
        for t in range(insts):
            traces = []
            for a in range(variables):
                rows = slice(8 * a, 8 * a + 8)
                picked = jnp.take_along_axis(
                    own_ref[t, rows, :], column, axis=1, mode="promise_in_bounds"
                )
                for mask, (_, ref, half) in zip(chosen, neighbours):
                    there = jnp.take_along_axis(
                        ref[half * insts + t, rows, :],
                        column,
                        axis=1,
                        mode="promise_in_bounds",
                    )
                    picked = jnp.where(mask, there, picked)
                traces.append(
                    jnp.take_along_axis(picked, corner, axis=0, mode="promise_in_bounds")
                )
            for a in range(0, variables, 2):
                start = 4 * a * stride + tile * insts + t
                if a + 1 < variables:
                    pair = jnp.where(row < 4, traces[a], traces[a + 1])
                    trace_ref[pl.ds(start, 8, stride=stride), :] = pair
                else:
                    trace_ref[pl.ds(start, 4, stride=stride), :] = traces[a][0:4, :]

    pair_rows = 2 * stride
    for i in range(width):
        total = None
        for p in range(width // 2):
            base = (i * width + 2 * p) * stride
            term = (
                blocks_ref[base : base + pair_rows, :]
                * trace_ref[p * pair_rows : (p + 1) * pair_rows, :]
            )
            total = term if total is None else total + term
        across_ref[i * pair_rows : (i + 1) * pair_rows, :] = total

    for tile in range(lane_tiles):
        place, held = within_of(wide(side_ref, tile), row)
        for t in range(insts):
            for a in range(variables):
                start = 4 * (a // 2) * 2 * pair_rows + tile * insts + t
                if a % 2 == 0:
                    here = across_ref[pl.ds(start, 8, stride=pair_rows), :]
                    here += across_ref[pl.ds(start + stride, 8, stride=pair_rows), :]
                moved = jnp.take_along_axis(
                    here, place + 4 * (a % 2), axis=0, mode="promise_in_bounds"
                )
                spread_ref[
                    (t * variables + a) * 8 : (t * variables + a) * 8 + 8,
                    tile * 128 : tile * 128 + 128,
                ] = jnp.where(held, moved, 0.0)

    slot = lax.broadcasted_iota(jnp.int32, (elements, 128), 0)
    owned = jnp.concatenate(
        [
            (jnp.broadcast_to(owner_ref[tile : tile + 1, :], slot.shape) == slot)
            for tile in range(lane_tiles)
        ],
        axis=1,
    )
    owned = jnp.where(owned, 1.0, 0.0).astype(jnp.bfloat16)
    spread = spread_ref[...]
    high = spread.astype(jnp.bfloat16)
    low = (spread - high.astype(jnp.float32)).astype(jnp.bfloat16)
    dims = (((1,), (1,)), ((), ()))
    landed = lax.dot_general(high, owned, dims, preferred_element_type=jnp.float32)
    landed += lax.dot_general(low, owned, dims, preferred_element_type=jnp.float32)

    live = lax.broadcasted_iota(jnp.int32, shape, 1) < counts_ref[0]
    mass = mass_ref[...]
    total_insts = insts * instances
    sources = (
        (own_ref, 0, 0, 0),
        (core_ref, 0, -1, 1),
        (chip_ref, 0, 2, 2),
        (chip_ref, insts, 1, -1),
    )
    for t in range(insts):
        element = element_term(own_ref, element_blocks_ref, t)
        for a in range(variables):
            rows = slice(8 * a, 8 * a + 8)
            summed = None
            for ref, base, ahead_first, ahead_second in sources:
                for s in range(insts):
                    even = spectral(t - s + insts * ahead_first, total_insts)
                    odd = spectral(t - s + insts * ahead_second, total_insts)
                    if even == 0.0 and odd == 0.0:
                        continue
                    weight = even if even == odd else jnp.where(on_first, even, odd)
                    term = weight * ref[base + s, rows, :]
                    summed = term if summed is None else summed + term
            base = (t * variables + a) * 8
            value = element[a] + landed[base : base + 8, :] + mass * summed
            out_ref[t, rows, :] = jnp.where(live, value, 0.0)


def jacobian_rows(
    keep, counts, place, owner, side, part, nbr, mass, element_blocks, blocks, own, *fields
):
    part_total = lax.axis_size("dom")
    instances = lax.axis_size("inst")
    insts, unknowns, _ = own.shape
    width = unknowns // 2
    stride = owner.shape[0] * insts
    vmem = pl.BlockSpec(memory_space=pltpu.VMEM)
    smem = pl.BlockSpec(memory_space=pltpu.SMEM)
    return pl.pallas_call(
        functools.partial(jacobian_kernel, instances, part_total),
        out_shape=(pltpu.VMEM if keep else jax.ShapeDtypeStruct)(own.shape, jnp.float32),
        in_specs=[smem, smem] + [vmem] * (8 + len(fields)),
        out_specs=vmem,
        scratch_shapes=[
            pltpu.VMEM((width * stride, 128), jnp.float32),
            pltpu.VMEM(((width + 4) * 2 * stride, 128), jnp.float32),
            pltpu.VMEM((insts * unknowns, owner.shape[0] * 128), jnp.float32),
        ],
        cost_estimate=pl.CostEstimate(
            flops=4 * blocks.size, bytes_accessed=4 * blocks.size, transcendentals=0
        ),
        compiler_params=pltpu.CompilerParams(vmem_limit_bytes=16 * 2**20),
    )(counts, place, owner, side, part, nbr, mass, element_blocks, blocks, own, *fields)


def on_device(
    state,
    element_jacobian_blocks,
    face_blocks,
    mass,
    counts,
    face_owner,
    face_side,
    face_part,
    face_nbr,
):
    tiles = face_blocks.shape[-1] // 128
    blocks = regroup(jnp.transpose(face_blocks, (1, 2, 0, 3)))
    owner, side, part, nbr = (
        x.reshape(tiles, 128) for x in (face_owner, face_side, face_part, face_nbr)
    )
    place = jnp.stack(
        [lax.axis_index("dom"), lax.axis_index("inst") % 2]
    ).astype(jnp.int32)

    def apply_jacobian(vector, keep):
        other = send(vector, to_core)
        both = pack(vector, other)
        far = send(both, to_far)
        near = send(both, to_near)
        chip = send(both, to_chip)
        other_near = send(near, to_core)
        other_far = send(far, to_core)
        return jacobian_rows(
            keep, counts, place, owner, side, part, nbr, mass, element_jacobian_blocks, blocks, vector,
            other, chip, far, near, other_far, other_near,
        )

    first = apply_jacobian(state, True)
    second = apply_jacobian(first, False)
    return first, second


def solution(mesh):
    placed = (
        P("inst", None, "dom"),
        P("inst", None, None, "dom"),
        P("inst", None, None, "dom"),
        P(None, "dom"),
        P("dom"),
        P("dom"),
        P("dom"),
        P("dom"),
        P("dom"),
    )
    return jax.shard_map(
        on_device,
        mesh=mesh,
        in_specs=placed,
        out_specs=(P("inst", None, "dom"), P("inst", None, "dom")),
        check_vma=False,
    )
```

```python
import functools
import math

import jax
import jax.numpy as jnp
from jax import lax
from jax.experimental import pallas as pl
from jax.experimental.pallas import tpu as pltpu
from jax.sharding import PartitionSpec as P

OMEGA = 1.0


def spectral(spacing, total):
    wrapped = spacing % total
    if wrapped == 0 or 2 * wrapped == total:
        return 0.0
    return 0.5 * OMEGA * (-1.0) ** wrapped / math.tan(math.pi * wrapped / total)


def joint(rule):
    insts, parts = lax.axis_size("inst"), lax.axis_size("dom")
    pairs = []
    for inst in range(insts):
        for part in range(parts):
            to_inst, to_part = rule(inst, part)
            pairs.append((inst * parts + part, to_inst * parts + to_part % parts))
    return pairs


def send(value, rule):
    return lax.ppermute(value, ("inst", "dom"), joint(rule))


def to_core(inst, part):
    return inst ^ 1, part


def to_chip(inst, part):
    return inst ^ 2, part


def near_step(part, reach):
    return -reach if part & reach else reach


def to_near(inst, part):
    return inst, part + near_step(part, 1 + inst % 2)


def to_far(inst, part):
    return inst, part - near_step(part, 1 + inst % 2)


def join_kernel(base, first_ref, second_ref, out_ref):
    insts = out_ref.shape[0] // 2
    out_ref[:insts] = first_ref[base : base + insts]
    out_ref[insts:] = second_ref[base : base + insts]


def join(first, second, base):
    insts = first.shape[0] - base
    return pl.pallas_call(
        functools.partial(join_kernel, base),
        out_shape=jax.ShapeDtypeStruct((2 * insts,) + first.shape[1:], jnp.float32),
        in_specs=[pl.BlockSpec(memory_space=pltpu.VMEM)] * 2,
        out_specs=pl.BlockSpec(memory_space=pltpu.VMEM),
        cost_estimate=pl.CostEstimate(
            flops=0, bytes_accessed=8 * first.size, transcendentals=0
        ),
        compiler_params=pltpu.CompilerParams(vmem_limit_bytes=2**20),
    )(first, second)


def sublanes():
    return lax.broadcasted_iota(jnp.int32, (8, 128), 0)


def fold_rows(tiles):
    row = sublanes()
    step = 1
    while len(tiles) > 1:
        keep = (row & step) == 0
        merged = []
        for first, second in zip(tiles[0::2], tiles[1::2]):
            own = jnp.where(keep, first, second)
            other = jnp.where(keep, second, first)
            merged.append(own + pltpu.roll(other, 8 - step, 0))
        tiles = merged
        step *= 2
    return tiles[0]


def element_term(vector_ref, blocks_ref, t):
    unknowns = vector_ref.shape[1]
    tiles = [vector_ref[t, 8 * g : 8 * g + 8, :] for g in range(unknowns // 8)]
    groups = []
    for group in range(unknowns // 8):
        partial = []
        for i in range(8 * group, 8 * group + 8):
            total = blocks_ref[t, i, 0:8, :] * tiles[0]
            for g in range(1, unknowns // 8):
                total += blocks_ref[t, i, 8 * g : 8 * g + 8, :] * tiles[g]
            partial.append(total)
        groups.append(fold_rows(partial))
    return groups


CHUNKS = 4


def stage_kernel(
    state_ref,
    element_ref,
    faces_ref,
    own_ref,
    element_out_ref,
    out_ref,
    held_ref,
    state_sem,
    element_sem,
    face_sems,
):
    rows, columns, insts, faces = faces_ref.shape
    lane_tiles = faces // 128
    stride = lane_tiles * insts
    depth = rows // CHUNKS
    copies = []
    for c in range(CHUNKS):
        part = pl.ds(c * depth, depth)
        copies.append(
            pltpu.make_async_copy(faces_ref.at[part], held_ref.at[part], face_sems.at[c])
        )
        copies[-1].start()
    state_copy = pltpu.make_async_copy(state_ref, own_ref, state_sem)
    state_copy.start()
    element_copy = pltpu.make_async_copy(element_ref, element_out_ref, element_sem)
    element_copy.start()

    def one_row(i, carry):
        base = pl.multiple_of(i * columns * stride, 8)
        for p in range(columns):
            for tile in range(lane_tiles):
                out_ref[pl.ds(base + p * stride + tile * insts, insts), :] = held_ref[
                    i, p, :, tile * 128 : tile * 128 + 128
                ]
        return carry

    for c in range(CHUNKS):
        copies[c].wait()
        lax.fori_loop(c * depth, (c + 1) * depth, one_row, 0)
    state_copy.wait()
    element_copy.wait()


def stage(state, element_blocks, face_blocks):
    anywhere = pl.BlockSpec(memory_space=pltpu.HBM)
    vmem = pl.BlockSpec(memory_space=pltpu.VMEM)
    return pl.pallas_call(
        stage_kernel,
        out_shape=(
            pltpu.VMEM(state.shape, jnp.float32),
            pltpu.VMEM(element_blocks.shape, jnp.float32),
            pltpu.VMEM((face_blocks.size // 128, 128), jnp.float32),
        ),
        in_specs=[anywhere] * 3,
        out_specs=(vmem, vmem, vmem),
        scratch_shapes=[
            pltpu.VMEM(face_blocks.shape, jnp.float32),
            pltpu.SemaphoreType.DMA,
            pltpu.SemaphoreType.DMA,
            pltpu.SemaphoreType.DMA((CHUNKS,)),
        ],
        cost_estimate=pl.CostEstimate(
            flops=0, bytes_accessed=4 * element_blocks.size, transcendentals=0
        ),
        compiler_params=pltpu.CompilerParams(vmem_limit_bytes=4 * 2**20),
    )(
        *(
            pltpu.with_memory_space_constraint(x, pltpu.HBM)
            for x in (state, element_blocks, face_blocks)
        )
    )


def corner_of(side, within):
    axis, end = side >> 1, side & 1
    return jnp.where(
        axis == 0,
        2 * within + end,
        jnp.where(
            axis == 1,
            (within & 1) + 2 * end + 4 * (within >> 1),
            4 * end + within,
        ),
    )


def within_of(side, corner):
    axis, end = side >> 1, side & 1
    place = jnp.where(
        axis == 0,
        corner >> 1,
        jnp.where(axis == 1, (corner & 1) + 2 * (corner >> 2), corner & 3),
    )
    held = ((corner >> axis) & 1) == end
    return place, held


def jacobian_kernel(
    instances,
    part_total,
    keep,
    counts_ref,
    owner_ref,
    side_ref,
    part_ref,
    nbr_ref,
    mass_ref,
    element_blocks_ref,
    blocks_ref,
    own_ref,
    core_ref,
    chip_ref,
    far_ref,
    near_ref,
    passed_ref,
    out_ref,
    *rest,
):
    trace_ref, across_ref, spread_ref = rest[-3:] if keep else rest[1:4]
    if not keep:
        save = pltpu.make_async_copy(own_ref, rest[0], rest[4])
        save.start()
    my_part = lax.axis_index("dom")
    on_first = (lax.axis_index("inst") & 1) == 0
    step_one = jnp.where((my_part & 1) == 0, 1, -1)
    step_two = jnp.where((my_part & 2) == 0, 2, -2)
    mine = jnp.where(on_first, step_one, step_two)
    others = jnp.where(on_first, step_two, step_one)
    neighbours = (
        (-mine, far_ref, 0),
        (mine, near_ref, 0),
        (-others, passed_ref, 0),
        (others, passed_ref, 1),
    )
    insts, unknowns, elements = own_ref.shape
    variables = unknowns // 8
    width = 4 * variables
    lane_tiles = owner_ref.shape[0]
    stride = lane_tiles * insts
    row = sublanes()
    shape = (8, 128)

    def wide(ref, tile):
        return jnp.broadcast_to(ref[tile : tile + 1, :], shape)

    for tile in range(lane_tiles):
        column = wide(nbr_ref, tile)
        offset = wide(part_ref, tile) - my_part
        offset = jnp.where(offset > 2, offset - part_total, offset)
        offset = jnp.where(offset < -2, offset + part_total, offset)
        chosen = [offset == o for o, _, _ in neighbours]
        corner = corner_of(wide(side_ref, tile) ^ 1, row & 3)
        for t in range(insts):
            traces = []
            for a in range(variables):
                rows = slice(8 * a, 8 * a + 8)
                picked = jnp.take_along_axis(
                    own_ref[t, rows, :], column, axis=1, mode="promise_in_bounds"
                )
                for mask, (_, ref, half) in zip(chosen, neighbours):
                    there = jnp.take_along_axis(
                        ref[half * insts + t, rows, :],
                        column,
                        axis=1,
                        mode="promise_in_bounds",
                    )
                    picked = jnp.where(mask, there, picked)
                traces.append(
                    jnp.take_along_axis(picked, corner, axis=0, mode="promise_in_bounds")
                )
            for a in range(0, variables, 2):
                start = 4 * a * stride + tile * insts + t
                if a + 1 < variables:
                    pair = jnp.where(row < 4, traces[a], traces[a + 1])
                    trace_ref[pl.ds(start, 8, stride=stride), :] = pair
                else:
                    trace_ref[pl.ds(start, 4, stride=stride), :] = traces[a][0:4, :]

    pair_rows = 2 * stride
    for i in range(width):
        total = None
        for p in range(width // 2):
            base = (i * width + 2 * p) * stride
            term = (
                blocks_ref[base : base + pair_rows, :]
                * trace_ref[p * pair_rows : (p + 1) * pair_rows, :]
            )
            total = term if total is None else total + term
        across_ref[i * pair_rows : (i + 1) * pair_rows, :] = total

    for tile in range(lane_tiles):
        place, held = within_of(wide(side_ref, tile), row)
        for t in range(insts):
            for a in range(variables):
                start = 4 * (a // 2) * 2 * pair_rows + tile * insts + t
                if a % 2 == 0:
                    here = across_ref[pl.ds(start, 8, stride=pair_rows), :]
                    here += across_ref[pl.ds(start + stride, 8, stride=pair_rows), :]
                moved = jnp.take_along_axis(
                    here, place + 4 * (a % 2), axis=0, mode="promise_in_bounds"
                )
                spread_ref[
                    (t * variables + a) * 8 : (t * variables + a) * 8 + 8,
                    tile * 128 : tile * 128 + 128,
                ] = jnp.where(held, moved, 0.0)

    slot = lax.broadcasted_iota(jnp.int32, (elements, 128), 0)
    owned = jnp.concatenate(
        [
            (jnp.broadcast_to(owner_ref[tile : tile + 1, :], slot.shape) == slot)
            for tile in range(lane_tiles)
        ],
        axis=1,
    )
    owned = jnp.where(owned, 1.0, 0.0).astype(jnp.bfloat16)
    spread = spread_ref[...]
    high = spread.astype(jnp.bfloat16)
    low = (spread - high.astype(jnp.float32)).astype(jnp.bfloat16)
    dims = (((1,), (1,)), ((), ()))
    landed = lax.dot_general(high, owned, dims, preferred_element_type=jnp.float32)
    landed += lax.dot_general(low, owned, dims, preferred_element_type=jnp.float32)

    live = lax.broadcasted_iota(jnp.int32, shape, 1) < counts_ref[...]
    mass = mass_ref[...]
    total_insts = insts * instances
    sources = (
        (own_ref, 0, 0, 0),
        (core_ref, 0, -1, 1),
        (chip_ref, 0, 2, 2),
        (chip_ref, insts, 1, -1),
    )
    for t in range(insts):
        element = element_term(own_ref, element_blocks_ref, t)
        for a in range(variables):
            rows = slice(8 * a, 8 * a + 8)
            summed = None
            for ref, base, ahead_first, ahead_second in sources:
                for s in range(insts):
                    even = spectral(t - s + insts * ahead_first, total_insts)
                    odd = spectral(t - s + insts * ahead_second, total_insts)
                    if even == 0.0 and odd == 0.0:
                        continue
                    weight = even if even == odd else jnp.where(on_first, even, odd)
                    term = weight * ref[base + s, rows, :]
                    summed = term if summed is None else summed + term
            base = (t * variables + a) * 8
            value = element[a] + landed[base : base + 8, :] + mass * summed
            out_ref[t, rows, :] = jnp.where(live, value, 0.0)
    if not keep:
        save.wait()


def jacobian_rows(
    keep, counts, owner, side, part, nbr, mass, element_blocks, blocks, own, *fields
):
    part_total = lax.axis_size("dom")
    instances = lax.axis_size("inst")
    insts, unknowns, _ = own.shape
    width = unknowns // 2
    stride = owner.shape[0] * insts
    vmem = pl.BlockSpec(memory_space=pltpu.VMEM)
    result = jax.ShapeDtypeStruct(own.shape, jnp.float32)
    return pl.pallas_call(
        functools.partial(jacobian_kernel, instances, part_total, keep),
        out_shape=pltpu.VMEM(own.shape, jnp.float32) if keep else (result, result),
        in_specs=[vmem] * (9 + len(fields)),
        out_specs=vmem if keep else (vmem, pl.BlockSpec(memory_space=pl.ANY)),
        scratch_shapes=[
            pltpu.VMEM((width * stride, 128), jnp.float32),
            pltpu.VMEM(((width + 4) * 2 * stride, 128), jnp.float32),
            pltpu.VMEM((insts * unknowns, owner.shape[0] * 128), jnp.float32),
        ]
        + ([] if keep else [pltpu.SemaphoreType.DMA]),
        cost_estimate=pl.CostEstimate(
            flops=4 * blocks.size, bytes_accessed=4 * blocks.size, transcendentals=0
        ),
        compiler_params=pltpu.CompilerParams(vmem_limit_bytes=8 * 2**20),
    )(counts, owner, side, part, nbr, mass, element_blocks, blocks, own, *fields)


def on_device(
    state,
    element_jacobian_blocks,
    face_blocks,
    mass,
    counts,
    face_owner,
    face_side,
    face_part,
    face_nbr,
):
    tiles = face_blocks.shape[-1] // 128
    owner, side, part, nbr = (
        x.reshape(tiles, 128) for x in (face_owner, face_side, face_part, face_nbr)
    )
    live_count = counts.reshape(1, 1)
    own, element_blocks, blocks = stage(
        state, element_jacobian_blocks, jnp.transpose(face_blocks, (1, 2, 0, 3))
    )

    def apply_jacobian(vector, core, keep):
        both = join(vector, core, 0)
        far = send(both, to_far)
        near = send(both, to_near)
        chip = send(both, to_chip)
        passed = send(join(far, near, vector.shape[0]), to_core)
        return jacobian_rows(
            keep, live_count, owner, side, part, nbr, mass, element_blocks,
            blocks, vector, core, chip, far, near, passed,
        )

    first = apply_jacobian(own, send(state, to_core), True)
    second, first = apply_jacobian(first, send(first, to_core), False)
    return first, second


def solution(mesh):
    placed = (
        P("inst", None, "dom"),
        P("inst", None, None, "dom"),
        P("inst", None, None, "dom"),
        P(None, "dom"),
        P("dom"),
        P("dom"),
        P("dom"),
        P("dom"),
        P("dom"),
    )
    return jax.shard_map(
        on_device,
        mesh=mesh,
        in_specs=placed,
        out_specs=(P("inst", None, "dom"), P("inst", None, "dom")),
        check_vma=False,
    )
```

```python
import functools
import math

import jax
import jax.numpy as jnp
from jax import lax
from jax.experimental import pallas as pl
from jax.experimental.pallas import tpu as pltpu
from jax.sharding import PartitionSpec as P

OMEGA = 1.0


def spectral(spacing, total):
    wrapped = spacing % total
    if wrapped == 0 or 2 * wrapped == total:
        return 0.0
    return 0.5 * OMEGA * (-1.0) ** wrapped / math.tan(math.pi * wrapped / total)


def joint(rule):
    insts, parts = lax.axis_size("inst"), lax.axis_size("dom")
    pairs = []
    for inst in range(insts):
        for part in range(parts):
            to_inst, to_part = rule(inst, part)
            pairs.append((inst * parts + part, to_inst * parts + to_part % parts))
    return pairs


def send(value, rule):
    return lax.ppermute(value, ("inst", "dom"), joint(rule))


def to_core(inst, part):
    return inst ^ 1, part


def to_chip(inst, part):
    return inst ^ 2, part


def near_step(part, reach):
    return -reach if part & reach else reach


def to_near(inst, part):
    return inst, part + near_step(part, 1 + inst % 2)


def to_far(inst, part):
    return inst, part - near_step(part, 1 + inst % 2)


def join_kernel(base, first_ref, second_ref, *rest):
    out_ref = rest[-1]
    insts = out_ref.shape[0] // 2
    out_ref[:insts] = first_ref[base : base + insts]
    out_ref[insts:] = second_ref[base : base + insts]


def join(first, second, base, *after):
    insts = first.shape[0] - base
    return pl.pallas_call(
        functools.partial(join_kernel, base),
        out_shape=jax.ShapeDtypeStruct((2 * insts,) + first.shape[1:], jnp.float32),
        in_specs=[pl.BlockSpec(memory_space=pltpu.VMEM)] * 2
        + [pl.BlockSpec(memory_space=pl.ANY)] * len(after),
        out_specs=pl.BlockSpec(memory_space=pltpu.VMEM),
        cost_estimate=pl.CostEstimate(
            flops=0, bytes_accessed=8 * first.size, transcendentals=0
        ),
        compiler_params=pltpu.CompilerParams(vmem_limit_bytes=2**20),
    )(first, second, *after)


def sublanes():
    return lax.broadcasted_iota(jnp.int32, (8, 128), 0)


def fold_rows(tiles):
    row = sublanes()
    step = 1
    while len(tiles) > 1:
        keep = (row & step) == 0
        merged = []
        for first, second in zip(tiles[0::2], tiles[1::2]):
            own = jnp.where(keep, first, second)
            other = jnp.where(keep, second, first)
            merged.append(own + pltpu.roll(other, 8 - step, 0))
        tiles = merged
        step *= 2
    return tiles[0]


def element_rows(vector_ref, blocks_ref, out_ref):
    insts, unknowns, _ = out_ref.shape
    for t in range(insts):
        tiles = [vector_ref[t, 8 * g : 8 * g + 8, :] for g in range(unknowns // 8)]
        for group in range(unknowns // 8):
            partial = []
            for i in range(8 * group, 8 * group + 8):
                total = blocks_ref[t, i, 0:8, :] * tiles[0]
                for g in range(1, unknowns // 8):
                    total += blocks_ref[t, i, 8 * g : 8 * g + 8, :] * tiles[g]
                partial.append(total)
            out_ref[t, 8 * group : 8 * group + 8, :] = fold_rows(partial)


def element_term(vector, blocks):
    return pl.pallas_call(
        element_rows,
        out_shape=jax.ShapeDtypeStruct(blocks.shape[:2] + blocks.shape[3:], jnp.float32),
        in_specs=[pl.BlockSpec(memory_space=pltpu.VMEM)] * 2,
        out_specs=pl.BlockSpec(memory_space=pltpu.VMEM),
        cost_estimate=pl.CostEstimate(
            flops=2 * blocks.size, bytes_accessed=4 * blocks.size, transcendentals=0
        ),
        compiler_params=pltpu.CompilerParams(vmem_limit_bytes=4 * 2**20),
    )(vector, blocks)


CHUNKS = 4


def fetch_kernel(source_ref, out_ref, sem):
    copy = pltpu.make_async_copy(source_ref, out_ref, sem)
    copy.start()
    copy.wait()


def fetch(value):
    return pl.pallas_call(
        fetch_kernel,
        out_shape=pltpu.VMEM(value.shape, jnp.float32),
        in_specs=[pl.BlockSpec(memory_space=pltpu.HBM)],
        out_specs=pl.BlockSpec(memory_space=pltpu.VMEM),
        scratch_shapes=[pltpu.SemaphoreType.DMA],
        cost_estimate=pl.CostEstimate(
            flops=0, bytes_accessed=8 * value.size, transcendentals=0
        ),
        compiler_params=pltpu.CompilerParams(vmem_limit_bytes=2**20),
    )(pltpu.with_memory_space_constraint(value, pltpu.HBM))


def stage_kernel(
    element_ref,
    faces_ref,
    both_ref,
    owner_ref,
    element_out_ref,
    out_ref,
    owned_ref,
    product_ref,
    held_ref,
    element_sem,
    face_sems,
):
    rows, columns, insts, faces = faces_ref.shape
    lane_tiles = faces // 128
    stride = lane_tiles * insts
    depth = rows // CHUNKS
    copies = []
    for c in range(CHUNKS):
        part = pl.ds(c * depth, depth)
        copies.append(
            pltpu.make_async_copy(faces_ref.at[part], held_ref.at[part], face_sems.at[c])
        )
        copies[-1].start()
    element_copy = pltpu.make_async_copy(element_ref, element_out_ref, element_sem)
    element_copy.start()

    slot = lax.broadcasted_iota(jnp.int32, (owned_ref.shape[0], 128), 0)
    owned = jnp.concatenate(
        [
            jnp.broadcast_to(owner_ref[tile : tile + 1, :], slot.shape) == slot
            for tile in range(lane_tiles)
        ],
        axis=1,
    )
    owned_ref[...] = jnp.where(owned, 1.0, 0.0).astype(jnp.bfloat16)

    def one_row(i, carry):
        base = pl.multiple_of(i * columns * stride, 8)
        for p in range(columns):
            for tile in range(lane_tiles):
                out_ref[pl.ds(base + p * stride + tile * insts, insts), :] = held_ref[
                    i, p, :, tile * 128 : tile * 128 + 128
                ]
        return carry

    for c in range(CHUNKS):
        copies[c].wait()
        lax.fori_loop(c * depth, (c + 1) * depth, one_row, 0)
    element_copy.wait()
    element_rows(both_ref, element_out_ref, product_ref)


def stage(element_blocks, face_blocks, both, owner):
    hbm = pl.BlockSpec(memory_space=pltpu.HBM)
    vmem = pl.BlockSpec(memory_space=pltpu.VMEM)
    insts, unknowns, _, elements = element_blocks.shape
    return pl.pallas_call(
        stage_kernel,
        out_shape=(
            pltpu.VMEM(element_blocks.shape, jnp.float32),
            pltpu.VMEM((face_blocks.size // 128, 128), jnp.float32),
            pltpu.VMEM((elements, owner.size), jnp.bfloat16),
            pltpu.VMEM((insts, unknowns, elements), jnp.float32),
        ),
        in_specs=[hbm, hbm, vmem, vmem],
        out_specs=(vmem, vmem, vmem, vmem),
        scratch_shapes=[
            pltpu.VMEM(face_blocks.shape, jnp.float32),
            pltpu.SemaphoreType.DMA,
            pltpu.SemaphoreType.DMA((CHUNKS,)),
        ],
        cost_estimate=pl.CostEstimate(
            flops=0, bytes_accessed=4 * element_blocks.size, transcendentals=0
        ),
        compiler_params=pltpu.CompilerParams(vmem_limit_bytes=4 * 2**20),
    )(
        pltpu.with_memory_space_constraint(element_blocks, pltpu.HBM),
        pltpu.with_memory_space_constraint(face_blocks, pltpu.HBM),
        both,
        owner,
    )


def corner_of(side, within):
    axis, end = side >> 1, side & 1
    return jnp.where(
        axis == 0,
        2 * within + end,
        jnp.where(
            axis == 1,
            (within & 1) + 2 * end + 4 * (within >> 1),
            4 * end + within,
        ),
    )


def within_of(side, corner):
    axis, end = side >> 1, side & 1
    place = jnp.where(
        axis == 0,
        corner >> 1,
        jnp.where(axis == 1, (corner & 1) + 2 * (corner >> 2), corner & 3),
    )
    held = ((corner >> axis) & 1) == end
    return place, held


def jacobian_kernel(
    instances,
    part_total,
    keep,
    counts_ref,
    owned_ref,
    side_ref,
    part_ref,
    nbr_ref,
    mass_ref,
    element_ref,
    blocks_ref,
    own_ref,
    core_ref,
    chip_ref,
    far_ref,
    near_ref,
    passed_ref,
    out_ref,
    *rest,
):
    trace_ref, across_ref, spread_ref = rest[-3:] if keep else rest[1:4]
    if not keep:
        save = pltpu.make_async_copy(own_ref, rest[0], rest[4])
        save.start()
    my_part = lax.axis_index("dom")
    on_first = (lax.axis_index("inst") & 1) == 0
    step_one = jnp.where((my_part & 1) == 0, 1, -1)
    step_two = jnp.where((my_part & 2) == 0, 2, -2)
    mine = jnp.where(on_first, step_one, step_two)
    others = jnp.where(on_first, step_two, step_one)
    neighbours = (
        (-mine, far_ref, 0),
        (mine, near_ref, 0),
        (-others, passed_ref, 0),
        (others, passed_ref, 1),
    )
    insts, unknowns, _ = own_ref.shape
    variables = unknowns // 8
    width = 4 * variables
    lane_tiles = side_ref.shape[0]
    stride = lane_tiles * insts
    row = sublanes()
    shape = (8, 128)

    def wide(ref, tile):
        return jnp.broadcast_to(ref[tile : tile + 1, :], shape)

    for tile in range(lane_tiles):
        column = wide(nbr_ref, tile)
        offset = wide(part_ref, tile) - my_part
        offset = jnp.where(offset > 2, offset - part_total, offset)
        offset = jnp.where(offset < -2, offset + part_total, offset)
        chosen = [offset == o for o, _, _ in neighbours]
        corner = corner_of(wide(side_ref, tile) ^ 1, row & 3)
        for t in range(insts):
            traces = []
            for a in range(variables):
                rows = slice(8 * a, 8 * a + 8)
                picked = jnp.take_along_axis(
                    own_ref[t, rows, :], column, axis=1, mode="promise_in_bounds"
                )
                for mask, (_, ref, half) in zip(chosen, neighbours):
                    there = jnp.take_along_axis(
                        ref[half * insts + t, rows, :],
                        column,
                        axis=1,
                        mode="promise_in_bounds",
                    )
                    picked = jnp.where(mask, there, picked)
                traces.append(
                    jnp.take_along_axis(picked, corner, axis=0, mode="promise_in_bounds")
                )
            for a in range(0, variables, 2):
                start = 4 * a * stride + tile * insts + t
                if a + 1 < variables:
                    pair = jnp.where(row < 4, traces[a], traces[a + 1])
                    trace_ref[pl.ds(start, 8, stride=stride), :] = pair
                else:
                    trace_ref[pl.ds(start, 4, stride=stride), :] = traces[a][0:4, :]

    pair_rows = 2 * stride
    for i in range(width):
        total = None
        for p in range(width // 2):
            base = (i * width + 2 * p) * stride
            term = (
                blocks_ref[base : base + pair_rows, :]
                * trace_ref[p * pair_rows : (p + 1) * pair_rows, :]
            )
            total = term if total is None else total + term
        across_ref[i * pair_rows : (i + 1) * pair_rows, :] = total

    for tile in range(lane_tiles):
        place, held = within_of(wide(side_ref, tile), row)
        for t in range(insts):
            for a in range(variables):
                start = 4 * (a // 2) * 2 * pair_rows + tile * insts + t
                if a % 2 == 0:
                    here = across_ref[pl.ds(start, 8, stride=pair_rows), :]
                    here += across_ref[pl.ds(start + stride, 8, stride=pair_rows), :]
                moved = jnp.take_along_axis(
                    here, place + 4 * (a % 2), axis=0, mode="promise_in_bounds"
                )
                spread_ref[
                    (t * variables + a) * 8 : (t * variables + a) * 8 + 8,
                    tile * 128 : tile * 128 + 128,
                ] = jnp.where(held, moved, 0.0)

    owned = owned_ref[...]
    spread = spread_ref[...]
    high = spread.astype(jnp.bfloat16)
    low = (spread - high.astype(jnp.float32)).astype(jnp.bfloat16)
    dims = (((1,), (1,)), ((), ()))
    landed = lax.dot_general(high, owned, dims, preferred_element_type=jnp.float32)
    landed += lax.dot_general(low, owned, dims, preferred_element_type=jnp.float32)

    live = lax.broadcasted_iota(jnp.int32, shape, 1) < counts_ref[...]
    mass = mass_ref[...]
    total_insts = insts * instances
    sources = (
        (own_ref, 0, 0, 0),
        (core_ref, 0, -1, 1),
        (chip_ref, 0, 2, 2),
        (chip_ref, insts, 1, -1),
    )
    for t in range(insts):
        for a in range(variables):
            rows = slice(8 * a, 8 * a + 8)
            summed = None
            for ref, base, ahead_first, ahead_second in sources:
                for s in range(insts):
                    even = spectral(t - s + insts * ahead_first, total_insts)
                    odd = spectral(t - s + insts * ahead_second, total_insts)
                    if even == 0.0 and odd == 0.0:
                        continue
                    weight = even if even == odd else jnp.where(on_first, even, odd)
                    term = weight * ref[base + s, rows, :]
                    summed = term if summed is None else summed + term
            base = (t * variables + a) * 8
            value = element_ref[t, rows, :] + landed[base : base + 8, :] + mass * summed
            out_ref[t, rows, :] = jnp.where(live, value, 0.0)
    if not keep:
        save.wait()


def jacobian_rows(
    keep, counts, owned, side, part, nbr, mass, element, blocks, own, *fields
):
    part_total = lax.axis_size("dom")
    instances = lax.axis_size("inst")
    insts, unknowns, _ = own.shape
    width = unknowns // 2
    stride = side.shape[0] * insts
    vmem = pl.BlockSpec(memory_space=pltpu.VMEM)
    result = jax.ShapeDtypeStruct(own.shape, jnp.float32)
    return pl.pallas_call(
        functools.partial(jacobian_kernel, instances, part_total, keep),
        out_shape=pltpu.VMEM(own.shape, jnp.float32) if keep else (result, result),
        in_specs=[vmem] * (9 + len(fields)),
        out_specs=vmem if keep else (vmem, pl.BlockSpec(memory_space=pl.ANY)),
        scratch_shapes=[
            pltpu.VMEM((width * stride, 128), jnp.float32),
            pltpu.VMEM(((width + 4) * 2 * stride, 128), jnp.float32),
            pltpu.VMEM((insts * unknowns, side.shape[0] * 128), jnp.float32),
        ]
        + ([] if keep else [pltpu.SemaphoreType.DMA]),
        cost_estimate=pl.CostEstimate(
            flops=4 * blocks.size, bytes_accessed=4 * blocks.size, transcendentals=0
        ),
        compiler_params=pltpu.CompilerParams(vmem_limit_bytes=8 * 2**20),
    )(counts, owned, side, part, nbr, mass, element, blocks, own, *fields)


def on_device(
    state,
    element_jacobian_blocks,
    face_blocks,
    mass,
    counts,
    face_owner,
    face_side,
    face_part,
    face_nbr,
):
    tiles = face_blocks.shape[-1] // 128
    owner, side, part, nbr = (
        x.reshape(tiles, 128) for x in (face_owner, face_side, face_part, face_nbr)
    )
    live_count = counts.reshape(1, 1)
    def exchange(both, *after):
        far = send(both, to_far)
        near = send(both, to_near)
        chip = send(both, to_chip)
        passed = send(join(far, near, both.shape[0] // 2, *after), to_core)
        return chip, far, near, passed

    core = send(state, to_core)
    own = fetch(state)
    both = join(own, core, 0)
    element_blocks, blocks, owned, element = stage(
        element_jacobian_blocks, jnp.transpose(face_blocks, (1, 2, 0, 3)), both, owner
    )
    first = jacobian_rows(
        True, live_count, owned, side, part, nbr, mass, element, blocks, own, core,
        *exchange(both, element),
    )

    core = send(first, to_core)
    element = element_term(first, element_blocks)
    second, first = jacobian_rows(
        False, live_count, owned, side, part, nbr, mass, element, blocks, first, core,
        *exchange(join(first, core, 0), element),
    )
    return first, second


def solution(mesh):
    placed = (
        P("inst", None, "dom"),
        P("inst", None, None, "dom"),
        P("inst", None, None, "dom"),
        P(None, "dom"),
        P("dom"),
        P("dom"),
        P("dom"),
        P("dom"),
        P("dom"),
    )
    return jax.shard_map(
        on_device,
        mesh=mesh,
        in_specs=placed,
        out_specs=(P("inst", None, "dom"), P("inst", None, "dom")),
        check_vma=False,
    )
```

```python
import functools
import math

import jax
import jax.numpy as jnp
from jax import lax
from jax.experimental import pallas as pl
from jax.experimental.pallas import tpu as pltpu
from jax.sharding import PartitionSpec as P

OMEGA = 1.0


def spectral(spacing, total):
    wrapped = spacing % total
    if wrapped == 0 or 2 * wrapped == total:
        return 0.0
    return 0.5 * OMEGA * (-1.0) ** wrapped / math.tan(math.pi * wrapped / total)


def joint(rule):
    insts, parts = lax.axis_size("inst"), lax.axis_size("dom")
    pairs = []
    for inst in range(insts):
        for part in range(parts):
            to_inst, to_part = rule(inst, part)
            pairs.append((inst * parts + part, to_inst * parts + to_part % parts))
    return pairs


def send(value, rule):
    return lax.ppermute(value, ("inst", "dom"), joint(rule))


def to_core(inst, part):
    return inst ^ 1, part


def to_chip(inst, part):
    return inst ^ 2, part


def near_step(part, reach):
    return -reach if part & reach else reach


def to_near(inst, part):
    return inst, part + near_step(part, 1 + inst % 2)


def to_far(inst, part):
    return inst, part - near_step(part, 1 + inst % 2)


def join_kernel(base, first_ref, second_ref, *rest):
    out_ref = rest[-1]
    insts = out_ref.shape[0] // 2
    out_ref[:insts] = first_ref[base : base + insts]
    out_ref[insts:] = second_ref[...]


def join(first, second, base, *after):
    insts = first.shape[0] - base
    return pl.pallas_call(
        functools.partial(join_kernel, base),
        out_shape=jax.ShapeDtypeStruct((2 * insts,) + first.shape[1:], jnp.float32),
        in_specs=[pl.BlockSpec(memory_space=pltpu.VMEM)] * 2
        + [pl.BlockSpec(memory_space=pl.ANY)] * len(after),
        out_specs=pl.BlockSpec(memory_space=pltpu.VMEM),
        cost_estimate=pl.CostEstimate(
            flops=0, bytes_accessed=8 * first.size, transcendentals=0
        ),
        compiler_params=pltpu.CompilerParams(vmem_limit_bytes=2**20),
    )(first, second, *after)


def second_half_kernel(both_ref, out_ref):
    out_ref[...] = both_ref[out_ref.shape[0] :]


def second_half(both):
    insts = both.shape[0] // 2
    return pl.pallas_call(
        second_half_kernel,
        out_shape=jax.ShapeDtypeStruct((insts,) + both.shape[1:], jnp.float32),
        in_specs=[pl.BlockSpec(memory_space=pltpu.VMEM)],
        out_specs=pl.BlockSpec(memory_space=pltpu.VMEM),
        cost_estimate=pl.CostEstimate(
            flops=0, bytes_accessed=4 * both.size, transcendentals=0
        ),
        compiler_params=pltpu.CompilerParams(vmem_limit_bytes=2**20),
    )(both)


def sublanes():
    return lax.broadcasted_iota(jnp.int32, (8, 128), 0)


def fold_rows(tiles):
    row = sublanes()
    step = 1
    while len(tiles) > 1:
        keep = (row & step) == 0
        merged = []
        for first, second in zip(tiles[0::2], tiles[1::2]):
            own = jnp.where(keep, first, second)
            other = jnp.where(keep, second, first)
            merged.append(own + pltpu.roll(other, 8 - step, 0))
        tiles = merged
        step *= 2
    return tiles[0]


def element_rows(vector_ref, blocks_ref, out_ref):
    insts, unknowns, _ = out_ref.shape
    for t in range(insts):
        tiles = [vector_ref[t, 8 * g : 8 * g + 8, :] for g in range(unknowns // 8)]
        for group in range(unknowns // 8):
            partial = []
            for i in range(8 * group, 8 * group + 8):
                total = blocks_ref[t, i, 0:8, :] * tiles[0]
                for g in range(1, unknowns // 8):
                    total += blocks_ref[t, i, 8 * g : 8 * g + 8, :] * tiles[g]
                partial.append(total)
            out_ref[t, 8 * group : 8 * group + 8, :] = fold_rows(partial)


def element_term(vector, blocks):
    return pl.pallas_call(
        element_rows,
        out_shape=jax.ShapeDtypeStruct(blocks.shape[:2] + blocks.shape[3:], jnp.float32),
        in_specs=[pl.BlockSpec(memory_space=pltpu.VMEM)] * 2,
        out_specs=pl.BlockSpec(memory_space=pltpu.VMEM),
        cost_estimate=pl.CostEstimate(
            flops=2 * blocks.size, bytes_accessed=4 * blocks.size, transcendentals=0
        ),
        compiler_params=pltpu.CompilerParams(vmem_limit_bytes=4 * 2**20),
    )(vector, blocks)


CHUNKS = 4


def fetch_kernel(source_ref, out_ref, sem):
    copy = pltpu.make_async_copy(source_ref, out_ref, sem)
    copy.start()
    copy.wait()


def fetch(value):
    return pl.pallas_call(
        fetch_kernel,
        out_shape=pltpu.VMEM(value.shape, jnp.float32),
        in_specs=[pl.BlockSpec(memory_space=pltpu.HBM)],
        out_specs=pl.BlockSpec(memory_space=pltpu.VMEM),
        scratch_shapes=[pltpu.SemaphoreType.DMA],
        cost_estimate=pl.CostEstimate(
            flops=0, bytes_accessed=8 * value.size, transcendentals=0
        ),
        compiler_params=pltpu.CompilerParams(vmem_limit_bytes=2**20),
    )(pltpu.with_memory_space_constraint(value, pltpu.HBM))


def stage_kernel(
    element_ref,
    faces_ref,
    both_ref,
    owner_ref,
    element_out_ref,
    out_ref,
    owned_ref,
    product_ref,
    held_ref,
    held_owner_ref,
    owner_sem,
    element_sem,
    face_sems,
):
    rows, columns, insts, faces = faces_ref.shape
    lane_tiles = faces // 128
    stride = lane_tiles * insts
    depth = rows // CHUNKS
    copies = []
    for c in range(CHUNKS):
        part = pl.ds(c * depth, depth)
        copies.append(
            pltpu.make_async_copy(faces_ref.at[part], held_ref.at[part], face_sems.at[c])
        )
        copies[-1].start()
    element_copy = pltpu.make_async_copy(element_ref, element_out_ref, element_sem)
    element_copy.start()

    owner_copy = pltpu.make_async_copy(owner_ref, held_owner_ref, owner_sem)
    owner_copy.start()
    owner_copy.wait()
    slot = lax.broadcasted_iota(jnp.int32, (owned_ref.shape[0], 128), 0)
    owned = jnp.concatenate(
        [
            jnp.broadcast_to(held_owner_ref[tile : tile + 1, :], slot.shape) == slot
            for tile in range(lane_tiles)
        ],
        axis=1,
    )
    owned_ref[...] = jnp.where(owned, 1.0, 0.0).astype(jnp.bfloat16)

    def one_row(i, carry):
        base = pl.multiple_of(i * columns * stride, 8)
        for p in range(columns):
            for tile in range(lane_tiles):
                out_ref[pl.ds(base + p * stride + tile * insts, insts), :] = held_ref[
                    i, p, :, tile * 128 : tile * 128 + 128
                ]
        return carry

    for c in range(CHUNKS):
        copies[c].wait()
        lax.fori_loop(c * depth, (c + 1) * depth, one_row, 0)
    element_copy.wait()
    element_rows(both_ref, element_out_ref, product_ref)


def stage(element_blocks, face_blocks, both, owner):
    hbm = pl.BlockSpec(memory_space=pltpu.HBM)
    vmem = pl.BlockSpec(memory_space=pltpu.VMEM)
    insts, unknowns, _, elements = element_blocks.shape
    return pl.pallas_call(
        stage_kernel,
        out_shape=(
            pltpu.VMEM(element_blocks.shape, jnp.float32),
            pltpu.VMEM((face_blocks.size // 128, 128), jnp.float32),
            pltpu.VMEM((elements, owner.size), jnp.bfloat16),
            pltpu.VMEM((insts, unknowns, elements), jnp.float32),
        ),
        in_specs=[hbm, hbm, vmem, hbm],
        out_specs=(vmem, vmem, vmem, vmem),
        scratch_shapes=[
            pltpu.VMEM(face_blocks.shape, jnp.float32),
            pltpu.VMEM(owner.shape, jnp.int32),
            pltpu.SemaphoreType.DMA,
            pltpu.SemaphoreType.DMA,
            pltpu.SemaphoreType.DMA((CHUNKS,)),
        ],
        cost_estimate=pl.CostEstimate(
            flops=0, bytes_accessed=4 * element_blocks.size, transcendentals=0
        ),
        compiler_params=pltpu.CompilerParams(vmem_limit_bytes=4 * 2**20),
    )(
        pltpu.with_memory_space_constraint(element_blocks, pltpu.HBM),
        pltpu.with_memory_space_constraint(face_blocks, pltpu.HBM),
        both,
        pltpu.with_memory_space_constraint(owner, pltpu.HBM),
    )


def corner_of(side, within):
    axis, end = side >> 1, side & 1
    return jnp.where(
        axis == 0,
        2 * within + end,
        jnp.where(
            axis == 1,
            (within & 1) + 2 * end + 4 * (within >> 1),
            4 * end + within,
        ),
    )


def within_of(side, corner):
    axis, end = side >> 1, side & 1
    place = jnp.where(
        axis == 0,
        corner >> 1,
        jnp.where(axis == 1, (corner & 1) + 2 * (corner >> 2), corner & 3),
    )
    held = ((corner >> axis) & 1) == end
    return place, held


def jacobian_kernel(
    instances,
    part_total,
    keep,
    counts_ref,
    owned_ref,
    side_ref,
    part_ref,
    nbr_ref,
    mass_ref,
    element_ref,
    blocks_ref,
    own_ref,
    core_ref,
    chip_ref,
    far_ref,
    near_ref,
    passed_ref,
    out_ref,
    *rest,
):
    trace_ref, across_ref, spread_ref = rest[-3:] if keep else rest[1:4]
    if not keep:
        save = pltpu.make_async_copy(own_ref, rest[0], rest[4])
        save.start()
    my_part = lax.axis_index("dom")
    on_first = (lax.axis_index("inst") & 1) == 0
    step_one = jnp.where((my_part & 1) == 0, 1, -1)
    step_two = jnp.where((my_part & 2) == 0, 2, -2)
    mine = jnp.where(on_first, step_one, step_two)
    others = jnp.where(on_first, step_two, step_one)
    neighbours = (
        (-mine, far_ref, 0),
        (mine, near_ref, 0),
        (-others, passed_ref, 0),
        (others, passed_ref, 1),
    )
    insts, unknowns, _ = own_ref.shape
    variables = unknowns // 8
    width = 4 * variables
    lane_tiles = side_ref.shape[0]
    stride = lane_tiles * insts
    row = sublanes()
    shape = (8, 128)

    def wide(ref, tile):
        return jnp.broadcast_to(ref[tile : tile + 1, :], shape)

    for tile in range(lane_tiles):
        column = wide(nbr_ref, tile)
        offset = wide(part_ref, tile) - my_part
        offset = jnp.where(offset > 2, offset - part_total, offset)
        offset = jnp.where(offset < -2, offset + part_total, offset)
        chosen = [offset == o for o, _, _ in neighbours]
        corner = corner_of(wide(side_ref, tile) ^ 1, row & 3)
        for t in range(insts):
            traces = []
            for a in range(variables):
                rows = slice(8 * a, 8 * a + 8)
                picked = jnp.take_along_axis(
                    own_ref[t, rows, :], column, axis=1, mode="promise_in_bounds"
                )
                for mask, (_, ref, half) in zip(chosen, neighbours):
                    there = jnp.take_along_axis(
                        ref[half * insts + t, rows, :],
                        column,
                        axis=1,
                        mode="promise_in_bounds",
                    )
                    picked = jnp.where(mask, there, picked)
                traces.append(
                    jnp.take_along_axis(picked, corner, axis=0, mode="promise_in_bounds")
                )
            for a in range(0, variables, 2):
                start = 4 * a * stride + tile * insts + t
                if a + 1 < variables:
                    pair = jnp.where(row < 4, traces[a], traces[a + 1])
                    trace_ref[pl.ds(start, 8, stride=stride), :] = pair
                else:
                    trace_ref[pl.ds(start, 4, stride=stride), :] = traces[a][0:4, :]

    pair_rows = 2 * stride
    for i in range(width):
        total = None
        for p in range(width // 2):
            base = (i * width + 2 * p) * stride
            term = (
                blocks_ref[base : base + pair_rows, :]
                * trace_ref[p * pair_rows : (p + 1) * pair_rows, :]
            )
            total = term if total is None else total + term
        across_ref[i * pair_rows : (i + 1) * pair_rows, :] = total

    for tile in range(lane_tiles):
        place, held = within_of(wide(side_ref, tile), row)
        for t in range(insts):
            for a in range(variables):
                start = 4 * (a // 2) * 2 * pair_rows + tile * insts + t
                if a % 2 == 0:
                    here = across_ref[pl.ds(start, 8, stride=pair_rows), :]
                    here += across_ref[pl.ds(start + stride, 8, stride=pair_rows), :]
                moved = jnp.take_along_axis(
                    here, place + 4 * (a % 2), axis=0, mode="promise_in_bounds"
                )
                spread_ref[
                    (t * variables + a) * 8 : (t * variables + a) * 8 + 8,
                    tile * 128 : tile * 128 + 128,
                ] = jnp.where(held, moved, 0.0)

    owned = owned_ref[...]
    spread = spread_ref[...]
    high = spread.astype(jnp.bfloat16)
    low = (spread - high.astype(jnp.float32)).astype(jnp.bfloat16)
    dims = (((1,), (1,)), ((), ()))
    landed = lax.dot_general(high, owned, dims, preferred_element_type=jnp.float32)
    landed += lax.dot_general(low, owned, dims, preferred_element_type=jnp.float32)

    live = lax.broadcasted_iota(jnp.int32, shape, 1) < counts_ref[...]
    mass = mass_ref[...]
    total_insts = insts * instances
    sources = (
        (own_ref, 0, 0, 0),
        (core_ref, 0, -1, 1),
        (chip_ref, 0, 2, 2),
        (chip_ref, insts, 1, -1),
    )
    for t in range(insts):
        for a in range(variables):
            rows = slice(8 * a, 8 * a + 8)
            summed = None
            for ref, base, ahead_first, ahead_second in sources:
                for s in range(insts):
                    even = spectral(t - s + insts * ahead_first, total_insts)
                    odd = spectral(t - s + insts * ahead_second, total_insts)
                    if even == 0.0 and odd == 0.0:
                        continue
                    weight = even if even == odd else jnp.where(on_first, even, odd)
                    term = weight * ref[base + s, rows, :]
                    summed = term if summed is None else summed + term
            base = (t * variables + a) * 8
            value = element_ref[t, rows, :] + landed[base : base + 8, :] + mass * summed
            out_ref[t, rows, :] = jnp.where(live, value, 0.0)
    if not keep:
        save.wait()


def jacobian_rows(
    keep, counts, owned, side, part, nbr, mass, element, blocks, own, *fields
):
    part_total = lax.axis_size("dom")
    instances = lax.axis_size("inst")
    insts, unknowns, _ = own.shape
    width = unknowns // 2
    stride = side.shape[0] * insts
    vmem = pl.BlockSpec(memory_space=pltpu.VMEM)
    result = jax.ShapeDtypeStruct(own.shape, jnp.float32)
    return pl.pallas_call(
        functools.partial(jacobian_kernel, instances, part_total, keep),
        out_shape=pltpu.VMEM(own.shape, jnp.float32) if keep else (result, result),
        in_specs=[vmem] * (9 + len(fields)),
        out_specs=vmem if keep else (vmem, pl.BlockSpec(memory_space=pl.ANY)),
        scratch_shapes=[
            pltpu.VMEM((width * stride, 128), jnp.float32),
            pltpu.VMEM(((width + 4) * 2 * stride, 128), jnp.float32),
            pltpu.VMEM((insts * unknowns, side.shape[0] * 128), jnp.float32),
        ]
        + ([] if keep else [pltpu.SemaphoreType.DMA]),
        cost_estimate=pl.CostEstimate(
            flops=4 * blocks.size, bytes_accessed=4 * blocks.size, transcendentals=0
        ),
        compiler_params=pltpu.CompilerParams(vmem_limit_bytes=8 * 2**20),
    )(counts, owned, side, part, nbr, mass, element, blocks, own, *fields)


def on_device(
    state,
    element_jacobian_blocks,
    face_blocks,
    mass,
    counts,
    face_owner,
    face_side,
    face_part,
    face_nbr,
):
    tiles = face_blocks.shape[-1] // 128
    owner, side, part, nbr = (
        x.reshape(tiles, 128) for x in (face_owner, face_side, face_part, face_nbr)
    )
    live_count = counts.reshape(1, 1)
    def exchange(both, *after):
        far = send(both, to_far)
        near = send(both, to_near)
        chip = send(both, to_chip)
        passed = send(join(far, second_half(near), both.shape[0] // 2, *after), to_core)
        return chip, far, near, passed

    core = send(state, to_core)
    own = fetch(state)
    both = join(own, core, 0)
    element_blocks, blocks, owned, element = stage(
        element_jacobian_blocks, jnp.transpose(face_blocks, (1, 2, 0, 3)), both, owner
    )
    first = jacobian_rows(
        True, live_count, owned, side, part, nbr, mass, element, blocks, own, core,
        *exchange(both, element),
    )

    core = send(first, to_core)
    element = element_term(first, element_blocks)
    second, first = jacobian_rows(
        False, live_count, owned, side, part, nbr, mass, element, blocks, first, core,
        *exchange(join(first, core, 0), element),
    )
    return first, second


def solution(mesh):
    placed = (
        P("inst", None, "dom"),
        P("inst", None, None, "dom"),
        P("inst", None, None, "dom"),
        P(None, "dom"),
        P("dom"),
        P("dom"),
        P("dom"),
        P("dom"),
        P("dom"),
    )
    return jax.shard_map(
        on_device,
        mesh=mesh,
        in_specs=placed,
        out_specs=(P("inst", None, "dom"), P("inst", None, "dom")),
        check_vma=False,
    )
```

```python
import functools
import math

import jax
import jax.numpy as jnp
from jax import lax
from jax.experimental import pallas as pl
from jax.experimental.pallas import tpu as pltpu
from jax.sharding import PartitionSpec as P

OMEGA = 1.0


def spectral(spacing, total):
    wrapped = spacing % total
    if wrapped == 0 or 2 * wrapped == total:
        return 0.0
    return 0.5 * OMEGA * (-1.0) ** wrapped / math.tan(math.pi * wrapped / total)


def joint(rule):
    insts, parts = lax.axis_size("inst"), lax.axis_size("dom")
    pairs = []
    for inst in range(insts):
        for part in range(parts):
            to_inst, to_part = rule(inst, part)
            pairs.append((inst * parts + part, to_inst * parts + to_part % parts))
    return pairs


def send(value, rule):
    return lax.ppermute(value, ("inst", "dom"), joint(rule))


def to_core(inst, part):
    return inst ^ 1, part


def to_chip(inst, part):
    return inst ^ 2, part


def near_step(part, reach):
    return -reach if part & reach else reach


def to_near(inst, part):
    return inst, part + near_step(part, 1 + inst % 2)


def to_far(inst, part):
    return inst, part - near_step(part, 1 + inst % 2)


def join_kernel(base, first_ref, second_ref, *rest):
    out_ref = rest[-1]
    insts = out_ref.shape[0] // 2
    out_ref[:insts] = first_ref[base : base + insts]
    out_ref[insts:] = second_ref[...]


def join(first, second, base, *after):
    insts = first.shape[0] - base
    return pl.pallas_call(
        functools.partial(join_kernel, base),
        out_shape=jax.ShapeDtypeStruct((2 * insts,) + first.shape[1:], jnp.float32),
        in_specs=[pl.BlockSpec(memory_space=pltpu.VMEM)] * 2
        + [pl.BlockSpec(memory_space=pl.ANY)] * len(after),
        out_specs=pl.BlockSpec(memory_space=pltpu.VMEM),
        cost_estimate=pl.CostEstimate(
            flops=0, bytes_accessed=8 * first.size, transcendentals=0
        ),
        compiler_params=pltpu.CompilerParams(vmem_limit_bytes=2**20),
    )(first, second, *after)


def second_half_kernel(both_ref, out_ref):
    out_ref[...] = both_ref[out_ref.shape[0] :]


def second_half(both):
    insts = both.shape[0] // 2
    return pl.pallas_call(
        second_half_kernel,
        out_shape=jax.ShapeDtypeStruct((insts,) + both.shape[1:], jnp.float32),
        in_specs=[pl.BlockSpec(memory_space=pltpu.VMEM)],
        out_specs=pl.BlockSpec(memory_space=pltpu.VMEM),
        cost_estimate=pl.CostEstimate(
            flops=0, bytes_accessed=4 * both.size, transcendentals=0
        ),
        compiler_params=pltpu.CompilerParams(vmem_limit_bytes=2**20),
    )(both)


def sublanes():
    return lax.broadcasted_iota(jnp.int32, (8, 128), 0)


def fold_rows(tiles):
    row = sublanes()
    step = 1
    while len(tiles) > 1:
        keep = (row & step) == 0
        merged = []
        for first, second in zip(tiles[0::2], tiles[1::2]):
            own = jnp.where(keep, first, second)
            other = jnp.where(keep, second, first)
            merged.append(own + pltpu.roll(other, 8 - step, 0))
        tiles = merged
        step *= 2
    return tiles[0]


def element_rows(vector_ref, blocks_ref, out_ref):
    insts, unknowns, _ = out_ref.shape
    for t in range(insts):
        tiles = [vector_ref[t, 8 * g : 8 * g + 8, :] for g in range(unknowns // 8)]
        for group in range(unknowns // 8):
            partial = []
            for i in range(8 * group, 8 * group + 8):
                total = blocks_ref[t, i, 0:8, :] * tiles[0]
                for g in range(1, unknowns // 8):
                    total += blocks_ref[t, i, 8 * g : 8 * g + 8, :] * tiles[g]
                partial.append(total)
            out_ref[t, 8 * group : 8 * group + 8, :] = fold_rows(partial)


def element_term(vector, blocks):
    return pl.pallas_call(
        element_rows,
        out_shape=jax.ShapeDtypeStruct(blocks.shape[:2] + blocks.shape[3:], jnp.float32),
        in_specs=[pl.BlockSpec(memory_space=pltpu.VMEM)] * 2,
        out_specs=pl.BlockSpec(memory_space=pltpu.VMEM),
        cost_estimate=pl.CostEstimate(
            flops=2 * blocks.size, bytes_accessed=4 * blocks.size, transcendentals=0
        ),
        compiler_params=pltpu.CompilerParams(vmem_limit_bytes=4 * 2**20),
    )(vector, blocks)


CHUNKS = 4


def fetch_kernel(source_ref, out_ref, sem):
    copy = pltpu.make_async_copy(source_ref, out_ref, sem)
    copy.start()
    copy.wait()


def fetch(value):
    return pl.pallas_call(
        fetch_kernel,
        out_shape=pltpu.VMEM(value.shape, jnp.float32),
        in_specs=[pl.BlockSpec(memory_space=pltpu.HBM)],
        out_specs=pl.BlockSpec(memory_space=pltpu.VMEM),
        scratch_shapes=[pltpu.SemaphoreType.DMA],
        cost_estimate=pl.CostEstimate(
            flops=0, bytes_accessed=8 * value.size, transcendentals=0
        ),
        compiler_params=pltpu.CompilerParams(vmem_limit_bytes=2**20),
    )(pltpu.with_memory_space_constraint(value, pltpu.HBM))


def stage_kernel(
    element_ref,
    faces_ref,
    both_ref,
    owner_ref,
    element_out_ref,
    out_ref,
    owned_ref,
    product_ref,
    held_ref,
    held_owner_ref,
    owner_sem,
    element_sem,
    face_sems,
):
    rows, columns, insts, faces = faces_ref.shape
    lane_tiles = faces // 128
    stride = lane_tiles * insts
    depth = rows // CHUNKS
    copies = []
    for c in range(CHUNKS):
        part = pl.ds(c * depth, depth)
        copies.append(
            pltpu.make_async_copy(faces_ref.at[part], held_ref.at[part], face_sems.at[c])
        )
        copies[-1].start()
    element_copy = pltpu.make_async_copy(element_ref, element_out_ref, element_sem)
    element_copy.start()

    owner_copy = pltpu.make_async_copy(owner_ref, held_owner_ref, owner_sem)
    owner_copy.start()
    owner_copy.wait()
    slot = lax.broadcasted_iota(jnp.int32, (owned_ref.shape[0], 128), 0)
    owned = jnp.concatenate(
        [
            jnp.broadcast_to(held_owner_ref[tile : tile + 1, :], slot.shape) == slot
            for tile in range(lane_tiles)
        ],
        axis=1,
    )
    owned_ref[...] = jnp.where(owned, 1.0, 0.0).astype(jnp.bfloat16)

    def one_row(i, carry):
        base = pl.multiple_of(i * columns * stride, 8)
        for p in range(columns):
            for tile in range(lane_tiles):
                out_ref[pl.ds(base + p * stride + tile * insts, insts), :] = held_ref[
                    i, p, :, tile * 128 : tile * 128 + 128
                ]
        return carry

    for c in range(CHUNKS):
        copies[c].wait()
        lax.fori_loop(c * depth, (c + 1) * depth, one_row, 0)
    element_copy.wait()
    element_rows(both_ref, element_out_ref, product_ref)


def stage(element_blocks, face_blocks, both, owner):
    hbm = pl.BlockSpec(memory_space=pltpu.HBM)
    vmem = pl.BlockSpec(memory_space=pltpu.VMEM)
    insts, unknowns, _, elements = element_blocks.shape
    return pl.pallas_call(
        stage_kernel,
        out_shape=(
            pltpu.VMEM(element_blocks.shape, jnp.float32),
            pltpu.VMEM((face_blocks.size // 128, 128), jnp.float32),
            pltpu.VMEM((elements, owner.size), jnp.bfloat16),
            pltpu.VMEM((insts, unknowns, elements), jnp.float32),
        ),
        in_specs=[hbm, hbm, vmem, hbm],
        out_specs=(vmem, vmem, vmem, vmem),
        scratch_shapes=[
            pltpu.VMEM(face_blocks.shape, jnp.float32),
            pltpu.VMEM(owner.shape, jnp.int32),
            pltpu.SemaphoreType.DMA,
            pltpu.SemaphoreType.DMA,
            pltpu.SemaphoreType.DMA((CHUNKS,)),
        ],
        cost_estimate=pl.CostEstimate(
            flops=0, bytes_accessed=4 * element_blocks.size, transcendentals=0
        ),
        compiler_params=pltpu.CompilerParams(vmem_limit_bytes=4 * 2**20),
    )(
        pltpu.with_memory_space_constraint(element_blocks, pltpu.HBM),
        pltpu.with_memory_space_constraint(face_blocks, pltpu.HBM),
        both,
        pltpu.with_memory_space_constraint(owner, pltpu.HBM),
    )


def corner_of(side, within):
    axis, end = side >> 1, side & 1
    return jnp.where(
        axis == 0,
        2 * within + end,
        jnp.where(
            axis == 1,
            (within & 1) + 2 * end + 4 * (within >> 1),
            4 * end + within,
        ),
    )


def within_of(side, corner):
    axis, end = side >> 1, side & 1
    place = jnp.where(
        axis == 0,
        corner >> 1,
        jnp.where(axis == 1, (corner & 1) + 2 * (corner >> 2), corner & 3),
    )
    held = ((corner >> axis) & 1) == end
    return place, held


def jacobian_kernel(
    instances,
    part_total,
    keep,
    counts_ref,
    owned_ref,
    side_ref,
    part_ref,
    nbr_ref,
    mass_ref,
    element_ref,
    blocks_ref,
    own_ref,
    core_ref,
    chip_ref,
    far_ref,
    near_ref,
    passed_ref,
    out_ref,
    *rest,
):
    trace_ref, across_ref, spread_ref = rest[-3:] if keep else rest[1:4]
    if not keep:
        save = pltpu.make_async_copy(own_ref, rest[0], rest[4])
        save.start()
        result_ref, out_ref = out_ref, rest[5]
        copies = []
    my_part = lax.axis_index("dom")
    on_first = (lax.axis_index("inst") & 1) == 0
    step_one = jnp.where((my_part & 1) == 0, 1, -1)
    step_two = jnp.where((my_part & 2) == 0, 2, -2)
    mine = jnp.where(on_first, step_one, step_two)
    others = jnp.where(on_first, step_two, step_one)
    neighbours = (
        (-mine, far_ref, 0),
        (mine, near_ref, 0),
        (-others, passed_ref, 0),
        (others, passed_ref, 1),
    )
    insts, unknowns, _ = own_ref.shape
    variables = unknowns // 8
    width = 4 * variables
    lane_tiles = side_ref.shape[0]
    stride = lane_tiles * insts
    row = sublanes()
    shape = (8, 128)

    def wide(ref, tile):
        return jnp.broadcast_to(ref[tile : tile + 1, :], shape)

    for tile in range(lane_tiles):
        column = wide(nbr_ref, tile)
        offset = wide(part_ref, tile) - my_part
        offset = jnp.where(offset > 2, offset - part_total, offset)
        offset = jnp.where(offset < -2, offset + part_total, offset)
        chosen = [offset == o for o, _, _ in neighbours]
        corner = corner_of(wide(side_ref, tile) ^ 1, row & 3)
        for t in range(insts):
            traces = []
            for a in range(variables):
                rows = slice(8 * a, 8 * a + 8)
                picked = jnp.take_along_axis(
                    own_ref[t, rows, :], column, axis=1, mode="promise_in_bounds"
                )
                for mask, (_, ref, half) in zip(chosen, neighbours):
                    there = jnp.take_along_axis(
                        ref[half * insts + t, rows, :],
                        column,
                        axis=1,
                        mode="promise_in_bounds",
                    )
                    picked = jnp.where(mask, there, picked)
                traces.append(
                    jnp.take_along_axis(picked, corner, axis=0, mode="promise_in_bounds")
                )
            for a in range(0, variables, 2):
                start = 4 * a * stride + tile * insts + t
                if a + 1 < variables:
                    pair = jnp.where(row < 4, traces[a], traces[a + 1])
                    trace_ref[pl.ds(start, 8, stride=stride), :] = pair
                else:
                    trace_ref[pl.ds(start, 4, stride=stride), :] = traces[a][0:4, :]

    pair_rows = 2 * stride
    for i in range(width):
        total = None
        for p in range(width // 2):
            base = (i * width + 2 * p) * stride
            term = (
                blocks_ref[base : base + pair_rows, :]
                * trace_ref[p * pair_rows : (p + 1) * pair_rows, :]
            )
            total = term if total is None else total + term
        across_ref[i * pair_rows : (i + 1) * pair_rows, :] = total

    for tile in range(lane_tiles):
        place, held = within_of(wide(side_ref, tile), row)
        for t in range(insts):
            for a in range(variables):
                start = 4 * (a // 2) * 2 * pair_rows + tile * insts + t
                if a % 2 == 0:
                    here = across_ref[pl.ds(start, 8, stride=pair_rows), :]
                    here += across_ref[pl.ds(start + stride, 8, stride=pair_rows), :]
                moved = jnp.take_along_axis(
                    here, place + 4 * (a % 2), axis=0, mode="promise_in_bounds"
                )
                spread_ref[
                    (t * variables + a) * 8 : (t * variables + a) * 8 + 8,
                    tile * 128 : tile * 128 + 128,
                ] = jnp.where(held, moved, 0.0)

    owned = owned_ref[...]
    spread = spread_ref[...]
    high = spread.astype(jnp.bfloat16)
    low = (spread - high.astype(jnp.float32)).astype(jnp.bfloat16)
    dims = (((1,), (1,)), ((), ()))
    landed = lax.dot_general(high, owned, dims, preferred_element_type=jnp.float32)
    landed += lax.dot_general(low, owned, dims, preferred_element_type=jnp.float32)

    live = lax.broadcasted_iota(jnp.int32, shape, 1) < counts_ref[...]
    mass = mass_ref[...]
    total_insts = insts * instances
    sources = (
        (own_ref, 0, 0, 0),
        (core_ref, 0, -1, 1),
        (chip_ref, 0, 2, 2),
        (chip_ref, insts, 1, -1),
    )
    for t in range(insts):
        for a in range(variables):
            rows = slice(8 * a, 8 * a + 8)
            summed = None
            for ref, base, ahead_first, ahead_second in sources:
                for s in range(insts):
                    even = spectral(t - s + insts * ahead_first, total_insts)
                    odd = spectral(t - s + insts * ahead_second, total_insts)
                    if even == 0.0 and odd == 0.0:
                        continue
                    weight = even if even == odd else jnp.where(on_first, even, odd)
                    term = weight * ref[base + s, rows, :]
                    summed = term if summed is None else summed + term
            base = (t * variables + a) * 8
            value = element_ref[t, rows, :] + landed[base : base + 8, :] + mass * summed
            out_ref[t, rows, :] = jnp.where(live, value, 0.0)
        if not keep:
            copies.append(
                pltpu.make_async_copy(out_ref.at[t], result_ref.at[t], rest[6].at[t])
            )
            copies[-1].start()
    if not keep:
        save.wait()
        for copy in copies:
            copy.wait()


def jacobian_rows(
    keep, counts, owned, side, part, nbr, mass, element, blocks, own, *fields
):
    part_total = lax.axis_size("dom")
    instances = lax.axis_size("inst")
    insts, unknowns, _ = own.shape
    width = unknowns // 2
    stride = side.shape[0] * insts
    vmem = pl.BlockSpec(memory_space=pltpu.VMEM)
    result = jax.ShapeDtypeStruct(own.shape, jnp.float32)
    return pl.pallas_call(
        functools.partial(jacobian_kernel, instances, part_total, keep),
        out_shape=pltpu.VMEM(own.shape, jnp.float32) if keep else (result, result),
        in_specs=[vmem] * (9 + len(fields)),
        out_specs=vmem if keep else (pl.BlockSpec(memory_space=pl.ANY),) * 2,
        scratch_shapes=[
            pltpu.VMEM((width * stride, 128), jnp.float32),
            pltpu.VMEM(((width + 4) * 2 * stride, 128), jnp.float32),
            pltpu.VMEM((insts * unknowns, side.shape[0] * 128), jnp.float32),
        ]
        + (
            []
            if keep
            else [
                pltpu.SemaphoreType.DMA,
                pltpu.VMEM(own.shape, jnp.float32),
                pltpu.SemaphoreType.DMA((insts,)),
            ]
        ),
        cost_estimate=pl.CostEstimate(
            flops=4 * blocks.size, bytes_accessed=4 * blocks.size, transcendentals=0
        ),
        compiler_params=pltpu.CompilerParams(vmem_limit_bytes=8 * 2**20),
    )(counts, owned, side, part, nbr, mass, element, blocks, own, *fields)


def on_device(
    state,
    element_jacobian_blocks,
    face_blocks,
    mass,
    counts,
    face_owner,
    face_side,
    face_part,
    face_nbr,
):
    tiles = face_blocks.shape[-1] // 128
    owner, side, part, nbr = (
        x.reshape(tiles, 128) for x in (face_owner, face_side, face_part, face_nbr)
    )
    live_count = counts.reshape(1, 1)
    def exchange(both, *after):
        far = send(both, to_far)
        near = send(both, to_near)
        chip = send(both, to_chip)
        passed = send(join(far, second_half(near), both.shape[0] // 2, *after), to_core)
        return chip, far, near, passed

    core = send(state, to_core)
    own = fetch(state)
    both = join(own, core, 0)
    element_blocks, blocks, owned, element = stage(
        element_jacobian_blocks, jnp.transpose(face_blocks, (1, 2, 0, 3)), both, owner
    )
    first = jacobian_rows(
        True, live_count, owned, side, part, nbr, mass, element, blocks, own, core,
        *exchange(both, element),
    )

    core = send(first, to_core)
    element = element_term(first, element_blocks)
    second, first = jacobian_rows(
        False, live_count, owned, side, part, nbr, mass, element, blocks, first, core,
        *exchange(join(first, core, 0), element),
    )
    return first, second


def solution(mesh):
    placed = (
        P("inst", None, "dom"),
        P("inst", None, None, "dom"),
        P("inst", None, None, "dom"),
        P(None, "dom"),
        P("dom"),
        P("dom"),
        P("dom"),
        P("dom"),
        P("dom"),
    )
    return jax.shard_map(
        on_device,
        mesh=mesh,
        in_specs=placed,
        out_specs=(P("inst", None, "dom"), P("inst", None, "dom")),
        check_vma=False,
    )
```
